128 devices in a mesh: clip: 16 (over z_hi, y, core), frame: 8 (over x, z_lo).
Axes of the slice: x: 4, y: 4, z: 4 (z_hi: 2, z_lo: 2; z = z_hi * 2 + z_lo), core: 2. Of those that a mesh axis runs over, the one named last changes fastest.
Arguments:
- latents: bfloat16 [128, 784, 640], P(('clip', 'frame')), may hold values from -6 to 6
- timestep: int32 [128], P(('clip', 'frame')), may hold values from 0 to 999
- ref_features: bfloat16 [784, 640], P('clip'), may hold values from -6 to 6
- norm_gains: float32 [3, 640], replicated, may hold values from 0.5 to 1.5
- w_spatial: bfloat16 [4, 640, 640], replicated, as said below
- w_temporal: bfloat16 [4, 640, 640], replicated, as said below
- w_time: bfloat16 [640, 1280], replicated, may hold values from -0.25 to 0.25
- w_in: bfloat16 [640, 5120], replicated, may hold values from -0.25 to 0.25
- w_out: bfloat16 [2560, 640], replicated, may hold values from -0.125 to 0.125
Outputs:
- result: bfloat16 [128, 784, 640], P(('clip', 'frame'))
The draws below stay inside these ranges and needn't reach their ends.
Inputs may be any that keep to these rules, and one draw needn't show every extreme that they name: `w_spatial`: query, key, value and output projections, in that order. `w_temporal`: query, key, value and output projections, in that order.
All inputs are finite; a program needn't handle non-finite values.
Results may differ from the reference program's by a relative error of at most 0.02.
Values may be sent and summed in bfloat16 or wider, within the bound.
A program may use at most 128 MiB of HBM per device.

```python
import math
import jax
import jax.numpy as jnp
from jax import lax

HEADS = 8
HEAD = 80
D = 640
FFH = 2560
P_SIZE = 784
FRAMES = 128
N_CLIP = 16
N_FRAME = 8


def attention_draw(key, query_scale, first_factor, second_factor):
    weights = jax.random.normal(key, (4, D, D), jnp.float32) * D ** (-0.5)
    columns = jnp.arange(D)
    factor = jnp.where(columns < HEAD, first_factor, jnp.where(columns < 2 * HEAD, second_factor, 0.0))
    query = weights[0] * query_scale
    keys = weights[1] + query * factor[None, :]
    return jnp.stack([query, keys, weights[2], weights[3]]).astype(jnp.bfloat16)


def draw_w_spatial(key, part):
    key = jax.random.fold_in(key, 11)
    return attention_draw(key, 2.5, 0.0, 0.0)


def draw_w_temporal(key, part):
    key = jax.random.fold_in(key, 23)
    return attention_draw(key, 1.5, 0.0, 0.0)


def touch_ends(drawn, key, smallest, top_value):
    place = [jax.random.randint(jax.random.fold_in(key, axis), (), 0, length) for axis, length in enumerate(drawn.shape)]
    main_axis = drawn.shape.index(max(drawn.shape))
    neighbour = place[:main_axis] + [(place[main_axis] + 1) % drawn.shape[main_axis]] + place[main_axis + 1:]
    return drawn.at[tuple(place)].set(smallest).at[tuple(neighbour)].set(top_value)


def steps_of(key, shape, shards, smallest, high):
    loudness = 1.0
    for dim, parts in shards:
        heights = jax.random.uniform(jax.random.fold_in(jax.random.fold_in(key, 6), dim), (parts,), jnp.float32, smallest / len(shards), high / len(shards))
        loudness = loudness * jnp.repeat(jnp.exp(heights), shape[dim] // parts).reshape((-1,) + (1,) * (len(shape) - 1 - dim))
    return loudness


def gaussian(key, dims, spread, most, shards=(), held_as=jnp.bfloat16):
    entries = jax.random.normal(key, dims, jnp.float32) * spread
    if len(shards) > 0:
        entries = steps_of(key, dims, shards, -0.22, 0.18) * entries
    return jnp.clip(entries, min=-most, max=most).astype(held_as)


def setup_inputs(seed: int = 0) -> dict:
    splits = jax.random.split(jax.random.key(seed), 10)
    latents = gaussian(splits[0], (FRAMES, P_SIZE, D), 1.0, 6.0, ((0, 128),))
    timestep = touch_ends(jax.random.randint(splits[1], (FRAMES,), 0, 1000), jax.random.fold_in(splits[1], 1), 0, 999).astype(jnp.int32)
    ref_features = gaussian(splits[2], (P_SIZE, D), 1.0, 6.0, ((0, 16),))
    norm_gains = jnp.clip(1.0 + 0.1 * jax.random.normal(splits[3], (3, D), jnp.float32), 0.5, 1.5)
    w_spatial = draw_w_spatial(jax.random.fold_in(splits[9], 71), 0)
    w_temporal = draw_w_temporal(jax.random.fold_in(splits[9], 71), 0)
    w_time = gaussian(splits[6], (D, 2 * D), D ** -0.5, 0.25)
    w_in = gaussian(splits[7], (D, 2 * FFH), D ** -0.5, 0.25)
    w_out = gaussian(splits[8], (FFH, D), FFH ** -0.5, 0.125)
    return {"latents": latents, "timestep": timestep, "ref_features": ref_features, "norm_gains": norm_gains, "w_spatial": w_spatial, "w_temporal": w_temporal, "w_time": w_time, "w_in": w_in, "w_out": w_out}


def layer_norm(values, gain):
    mean = lax.optimization_barrier(jnp.mean(values, axis=-1, keepdims=True))
    centered = values - mean
    variance = lax.optimization_barrier(jnp.mean(centered * centered, axis=-1, keepdims=True))
    return centered * lax.rsqrt(variance + 1e-05) * gain

def head_attention(query, keys, values):
    rows = query.shape[0]
    count = keys.shape[0]
    split_q = query.reshape(rows, HEADS, HEAD).transpose(1, 0, 2)
    split_k = keys.reshape(count, HEADS, HEAD).transpose(1, 0, 2)
    split_v = values.reshape(count, HEADS, HEAD).transpose(1, 0, 2)
    factor = 1.0 / math.sqrt(HEAD)

    def one_head(operands):
        head_q, head_k, head_v = operands
        scores = jnp.dot(head_q, head_k.T, preferred_element_type=jnp.float32) * factor
        top = lax.optimization_barrier(jnp.max(scores, axis=-1, keepdims=True))
        expo = jnp.exp(scores - top)
        weights = (expo / lax.optimization_barrier(jnp.sum(expo, axis=-1, keepdims=True))).astype(jnp.bfloat16)
        return jnp.dot(weights, head_v, preferred_element_type=jnp.float32).astype(jnp.bfloat16)
    outputs = lax.map(one_head, (split_q, split_k, split_v))
    return outputs.transpose(1, 0, 2).reshape(rows, HEADS * HEAD)

def temporal_attention(query, keys, values):
    frames, rows, width = query.shape
    head_q = query.reshape(frames, rows, HEADS, HEAD).astype(jnp.float32)
    head_k = keys.reshape(frames, rows, HEADS, HEAD).astype(jnp.float32)
    head_v = values.reshape(frames, rows, HEADS, HEAD).astype(jnp.float32)
    scores = jnp.einsum('fnhd,gnhd->nhfg', head_q, head_k) * (1.0 / math.sqrt(HEAD))
    top = lax.optimization_barrier(jnp.max(scores, axis=-1, keepdims=True))
    expo = jnp.exp(scores - top)
    weights = (expo / lax.optimization_barrier(jnp.sum(expo, axis=-1, keepdims=True))).astype(jnp.bfloat16)
    mixed = jnp.einsum('nhfg,gnhd->fnhd', weights.astype(jnp.float32), head_v)
    return mixed.astype(jnp.bfloat16).reshape(frames, rows, width)

def time_embedding(steps):
    half = D // 2
    freqs = jnp.exp(-math.log(10000.0) * jnp.arange(half, dtype=jnp.float32) / half)
    angles = steps.astype(jnp.float32)[:, None] * freqs[None, :]
    return jnp.concatenate([jnp.cos(angles), jnp.sin(angles)], axis=-1).astype(jnp.bfloat16)

def reference(latents, timestep, ref_features, norm_gains, w_spatial, w_temporal, w_time, w_in, w_out):
    w_pair = jnp.concatenate([w_spatial[1], w_spatial[2]], axis=1)
    ref_kv = jnp.dot(ref_features, w_pair, preferred_element_type=jnp.float32).astype(jnp.bfloat16)

    def spatial(frame):
        wide = frame.astype(jnp.float32)
        normed = layer_norm(wide, norm_gains[0]).astype(jnp.bfloat16)
        query = jnp.dot(normed, w_spatial[0], preferred_element_type=jnp.float32).astype(jnp.bfloat16)
        self_kv = jnp.dot(normed, w_pair, preferred_element_type=jnp.float32).astype(jnp.bfloat16)
        joined = jnp.concatenate([self_kv, ref_kv], axis=0)
        attended = head_attention(query, joined[:, :D], joined[:, D:])
        return (wide + jnp.dot(attended, w_spatial[3], preferred_element_type=jnp.float32)).astype(jnp.bfloat16)
    first = lax.map(spatial, latents)
    modulation = jnp.dot(time_embedding(timestep), w_time, preferred_element_type=jnp.float32)
    shift = modulation[:, :D]
    scale = modulation[:, D:]
    normed_two = (layer_norm(first.astype(jnp.float32), norm_gains[1]) * (1.0 + scale[:, None, :]) + shift[:, None, :]).astype(jnp.bfloat16)
    groups = normed_two.reshape(N_CLIP, N_FRAME, P_SIZE, D)

    def temporal(group):
        flat = group.reshape(N_FRAME * P_SIZE, D)
        query = jnp.dot(flat, w_temporal[0], preferred_element_type=jnp.float32).astype(jnp.bfloat16).reshape(N_FRAME, P_SIZE, D)
        keys = jnp.dot(flat, w_temporal[1], preferred_element_type=jnp.float32).astype(jnp.bfloat16).reshape(N_FRAME, P_SIZE, D)
        values = jnp.dot(flat, w_temporal[2], preferred_element_type=jnp.float32).astype(jnp.bfloat16).reshape(N_FRAME, P_SIZE, D)
        attended = temporal_attention(query, keys, values).reshape(N_FRAME * P_SIZE, D)
        return jnp.dot(attended, w_temporal[3], preferred_element_type=jnp.float32).astype(jnp.bfloat16).reshape(N_FRAME, P_SIZE, D)
    moved = lax.map(temporal, groups).reshape(FRAMES, P_SIZE, D)
    second = (first.astype(jnp.float32) + moved.astype(jnp.float32)).astype(jnp.bfloat16)

    def feed(frame):
        wide = frame.astype(jnp.float32)
        normed = layer_norm(wide, norm_gains[2]).astype(jnp.bfloat16)
        proj = jnp.dot(normed, w_in, preferred_element_type=jnp.float32)
        inner = (proj[:, :FFH] * jax.nn.gelu(proj[:, FFH:], approximate=False)).astype(jnp.bfloat16)
        return (wide + jnp.dot(inner, w_out, preferred_element_type=jnp.float32)).astype(jnp.bfloat16)
    return lax.map(feed, second)
```

```python
import math

import jax
import jax.numpy as jnp
from jax import lax
from jax.experimental import pallas as pl
from jax.experimental.pallas import tpu as pltpu
from jax.sharding import PartitionSpec as P

HEADS = 8
HEAD = 80
D = 640
FFH = 2560
ROWS = 784
PAD = 128
WIDE = HEADS * PAD
CLIP = 16
FRAME = 8
OWNERS = 7
BLOCK = 112
REF = 49
REF_PAD = 64
KEYS_SELF = 768
KEYS_REF = CLIP * REF_PAD
HALVES = ((0, 64, 0), (448, 48, 64))
LOG2E = 1.4426950408889634
FACTOR = LOG2E / math.sqrt(HEAD)
F32 = jnp.float32
BF16 = jnp.bfloat16
MESH = pl.DeviceIdType.MESH


def dot(a, b):
    return jnp.dot(a, b, preferred_element_type=F32)


def norm(wide):
    mean = jnp.mean(wide, axis=-1, keepdims=True)
    centered = wide - mean
    variance = jnp.mean(centered * centered, axis=-1, keepdims=True)
    return centered * lax.rsqrt(variance + 1e-05)


def iota(shape, axis):
    return lax.broadcasted_iota(jnp.int32, shape, axis)


def head_of(column):
    return (column * 52429) >> 22


def body(
    lat, ref, emb, gains, w_spatial, w_temporal, w_time, w_in, w_out, out,
    x, first, h, q, k_t, v, ref_stage, ref_all, kr_t, vr, acc, attn, wq, wk, wv, wo,
    ws, wt, wtime, win, wout, mod, spread, gather,
    recv_a, recv_b, tq, tk, tv, mixed, moved_a, moved_b, ret, inner, result,
    sem_x, sem_w, sem_out, ref_send, ref_recv, go_send, go_recv, back_send, back_recv,
):
    me_c = lax.axis_index("clip")
    me_f = lax.axis_index("frame")

    loads_x = []
    for half, (start, count, inside) in enumerate(HALVES):
        for j in range(OWNERS):
            loads_x.append(
                pltpu.make_async_copy(
                    lat.at[pl.ds(BLOCK * j + inside, count)],
                    x.at[pl.ds(start + count * j, count)],
                    sem_x.at[half * OWNERS + j],
                )
            )
    load_ws = pltpu.make_async_copy(w_spatial, ws, sem_w.at[0])
    load_wtime = pltpu.make_async_copy(w_time, wtime, sem_w.at[1])
    load_wt = pltpu.make_async_copy(w_temporal, wt, sem_w.at[2])
    load_win = pltpu.make_async_copy(w_in, win, sem_w.at[3])
    load_wout = pltpu.make_async_copy(w_out, wout, sem_w.at[4])
    for load in loads_x:
        load.start()
    load_ws.start()
    load_wtime.start()
    load_wt.start()
    load_win.start()
    load_wout.start()

    ref_stage[...] = jnp.zeros_like(ref_stage)
    ref_stage[0:REF, :] = ref[...]

    barrier = pltpu.get_barrier_semaphore()

    @pl.loop(1, CLIP)
    def _(d):
        pl.semaphore_signal(
            barrier, inc=1, device_id={"clip": lax.rem(me_c + d, CLIP)}, device_id_type=MESH
        )

    @pl.loop(1, FRAME)
    def _(d):
        pl.semaphore_signal(
            barrier, inc=1, device_id={"frame": lax.rem(me_f + d, FRAME)}, device_id_type=MESH
        )

    pl.semaphore_wait(barrier, CLIP + FRAME - 2)

    def ref_copy(d):
        return pltpu.make_async_remote_copy(
            src_ref=ref_stage,
            dst_ref=ref_all.at[pl.ds(pl.multiple_of(me_c * REF_PAD, REF_PAD), REF_PAD)],
            send_sem=ref_send.at[d],
            recv_sem=ref_recv.at[d],
            device_id={"clip": lax.rem(me_c + d, CLIP)},
            device_id_type=MESH,
        )

    @pl.loop(1, CLIP)
    def _(d):
        ref_copy(d).start()

    ref_all[pl.ds(pl.multiple_of(me_c * REF_PAD, REF_PAD), REF_PAD), :] = ref_stage[...]

    load_ws.wait()
    wq[...] = jnp.zeros_like(wq)
    wk[...] = jnp.zeros_like(wk)
    wv[...] = jnp.zeros_like(wv)
    wo[...] = jnp.zeros_like(wo)
    for i, target in enumerate((wq, wk, wv)):
        for n in range(HEADS):
            target[:, PAD * n : PAD * n + HEAD] = ws[i, :, HEAD * n : HEAD * n + HEAD]
    for n in range(HEADS):
        wo[PAD * n : PAD * n + HEAD, :] = ws[3, HEAD * n : HEAD * n + HEAD, :]

    for load in loads_x:
        load.wait()

    @pl.loop(0, ROWS // BLOCK)
    def _(i):
        rows = pl.ds(pl.multiple_of(i * BLOCK, BLOCK), BLOCK)
        h[rows, :] = (norm(x[rows, :].astype(F32)) * gains[0:1, :]).astype(BF16)

    @pl.loop(0, WIDE // 256)
    def _(j):
        c = pl.ds(pl.multiple_of(j * 256, 256), 256)
        lane = iota((1, 256), 1) & (PAD - 1)
        q[:, c] = jnp.where(lane == HEAD, 1.0, dot(h[...], wq[:, c]) * FACTOR).astype(BF16)
        k_t[c, :] = dot(h[0:KEYS_SELF, :], wk[:, c]).astype(BF16).T
        v[:, c] = jnp.where(lane == HEAD, 1.0, dot(h[0:KEYS_SELF, :], wv[:, c])).astype(BF16)

    @pl.loop(0, HEADS)
    def _(n):
        c = pl.ds(pl.multiple_of(n * PAD, PAD), PAD)
        s = dot(q[:, c], k_t[c, :])
        top = jnp.max(s, axis=1, keepdims=True)
        o = dot(jnp.exp2(s - top).astype(BF16), v[:, c])
        acc[:, c] = jnp.where(iota((1, PAD), 1) == HEAD + 1, top, o)

    load_wtime.wait()
    mod[...] = dot(emb[...], wtime[...])

    @pl.loop(0, FRAME)
    def _(g):
        lane = iota((D, PAD), 1) & (HEADS * FRAME - 1)
        gather[g] = (lane == FRAME * g + head_of(iota((D, PAD), 0))).astype(F32).astype(BF16)
        spread[g] = (
            (iota((PAD, D), 0) == FRAME * g + head_of(iota((PAD, D), 1))).astype(F32).astype(BF16)
        )

    @pl.loop(1, CLIP)
    def _(d):
        ref_copy(d).wait_recv()

    row = iota((PAD, 16), 0)
    tail = iota((PAD, 16), 1)
    place = ((row < REF_PAD) & (row == tail + REF)) | ((row == REF_PAD + REF) & (tail == 15))
    placed = dot(place.astype(F32).astype(BF16), h[KEYS_SELF:ROWS, :])
    ref_all[0:PAD, :] = (ref_all[0:PAD, :].astype(F32) + placed).astype(BF16)

    @pl.loop(0, WIDE // 256)
    def _(j):
        c = pl.ds(pl.multiple_of(j * 256, 256), 256)
        lane = iota((1, 256), 1) & (PAD - 1)
        key = iota((KEYS_REF, 1), 0)
        valid = ((key & (REF_PAD - 1)) < REF) | (key < REF_PAD) | (key == REF_PAD + REF)
        mask = jnp.where(valid, 0.0, -1e30)
        kr_t[c, :] = jnp.where(lane == HEAD, mask, dot(ref_all[...], wk[:, c])).astype(BF16).T
        vr[:, c] = jnp.where(lane == HEAD, 1.0, dot(ref_all[...], wv[:, c])).astype(BF16)

    def go_copy(half, d):
        start, count, _ = HALVES[half]
        target = lax.rem(me_f + d, FRAME)
        block = lax.min(target, OWNERS - 1)
        return pltpu.make_async_remote_copy(
            src_ref=h.at[pl.ds(pl.multiple_of(start + block * count, 16), count)],
            dst_ref=(recv_a, recv_b)[half].at[me_f],
            send_sem=go_send.at[half * FRAME + d],
            recv_sem=go_recv.at[half * FRAME + d],
            device_id={"frame": target},
            device_id_type=MESH,
        )

    def is_owner(d):
        return lax.rem(me_f + d, FRAME) < OWNERS

    def comes_from_owner(d):
        return lax.rem(me_f + FRAME - d, FRAME) < OWNERS

    for half, (start, count, _) in enumerate(HALVES):
        size = count * OWNERS
        rows = pl.ds(start, size)

        @pl.loop(0, HEADS)
        def _(n):
            c = pl.ds(pl.multiple_of(n * PAD, PAD), PAD)
            s = dot(q[rows, c], kr_t[c, :])
            top_r = jnp.max(s, axis=1, keepdims=True)
            o_r = dot(jnp.exp2(s - top_r).astype(BF16), vr[:, c])
            o_s = acc[rows, c]
            top_s = o_s[:, HEAD + 1 : HEAD + 2]
            top = jnp.maximum(top_r, top_s)
            o = o_s * jnp.exp2(top_s - top) + o_r * jnp.exp2(top_r - top)
            attn[0:size, c] = (o / o[:, HEAD : HEAD + 1]).astype(BF16)

        for c0, c1 in ((0, 256), (256, 512), (512, D)):
            first[rows, c0:c1] = (
                x[rows, c0:c1].astype(F32) + dot(attn[0:size, :], wo[:, c0:c1])
            ).astype(BF16)

        @pl.loop(0, OWNERS)
        def _(i):
            part = pl.ds(pl.multiple_of(start + i * count, 16), count)
            normed = norm(first[part, :].astype(F32)) * gains[1:2, :]
            h[part, :] = (normed * (1.0 + mod[0:1, D:]) + mod[0:1, :D]).astype(BF16)

        @pl.loop(1, FRAME)
        def _(d):
            @pl.when(is_owner(d))
            def _():
                go_copy(half, d).start()

        @pl.when(me_f < OWNERS)
        def _():
            (recv_a, recv_b)[half][me_f] = h[
                pl.ds(pl.multiple_of(start + lax.min(me_f, OWNERS - 1) * count, 16), count), :
            ]

    def back_copy(half, d):
        start, count, _ = HALVES[half]
        target = lax.rem(me_f + d, FRAME)
        return pltpu.make_async_remote_copy(
            src_ref=(moved_a, moved_b)[half].at[target],
            dst_ref=ret.at[pl.ds(pl.multiple_of(start + lax.min(me_f, OWNERS - 1) * count, 16), count)],
            send_sem=back_send.at[half * FRAME + d],
            recv_sem=back_recv.at[half * FRAME + d],
            device_id={"frame": target},
            device_id_type=MESH,
        )

    load_wt.wait()

    @pl.when(me_f < OWNERS)
    def _():
        for half, (start, count, _) in enumerate(HALVES):
            size = count * FRAME
            recv = (recv_a, recv_b)[half]
            moved = (moved_a, moved_b)[half]

            @pl.loop(1, FRAME)
            def _(d):
                go_copy(half, d).wait_recv()

            for c0, c1 in ((0, 256), (256, 512), (512, D)):
                states = recv[...].reshape(size, D)
                tq[0:size, c0:c1] = (dot(states, wt[0, :, c0:c1]) * FACTOR).astype(BF16)
                tk[0:size, c0:c1] = dot(states, wt[1, :, c0:c1]).astype(BF16)
                tv[0:size, c0:c1] = dot(states, wt[2, :, c0:c1]).astype(BF16)

            s = jnp.zeros((size, PAD), F32)
            for g in range(FRAME):
                keys = tk[g * count : (g + 1) * count, :]
                pairs = tq[0:size, :].reshape(FRAME, count, D) * keys[None]
                s = s + dot(pairs.reshape(size, D), gather[g])
            top = s
            for shift in (8, 16, 32):
                top = jnp.maximum(top, pltpu.roll(top, shift, 1))
            e = jnp.exp2(s - top)
            total = e
            for shift in (8, 16, 32):
                total = total + pltpu.roll(total, shift, 1)
            weights = (e / total).astype(BF16)
            for c0, c1 in ((0, 256), (256, 512), (512, D)):
                sums = jnp.zeros((FRAME, count, c1 - c0), F32)
                for g in range(FRAME):
                    values = tv[g * count : (g + 1) * count, c0:c1].astype(F32)
                    wide = dot(weights, spread[g, :, c0:c1]).reshape(FRAME, count, c1 - c0)
                    sums = sums + wide * values[None]
                mixed[0:size, c0:c1] = sums.reshape(size, c1 - c0).astype(BF16)
            for c0, c1 in ((0, 256), (256, 512), (512, D)):
                moved[:, :, c0:c1] = (
                    dot(mixed[0:size, :], wt[3, :, c0:c1]).astype(BF16).reshape(FRAME, count, c1 - c0)
                )

            @pl.loop(1, FRAME)
            def _(d):
                back_copy(half, d).start()

            ret[pl.ds(pl.multiple_of(start + lax.min(me_f, OWNERS - 1) * count, 16), count), :] = moved[
                me_f
            ]

    load_win.wait()
    load_wout.wait()
    stores = []
    for half, (start, count, inside) in enumerate(HALVES):
        size = count * OWNERS
        rows = pl.ds(start, size)

        @pl.loop(1, FRAME)
        def _(d):
            @pl.when(comes_from_owner(d))
            def _():
                back_copy(half, d).wait_recv()

        @pl.loop(0, OWNERS)
        def _(i):
            part = pl.ds(pl.multiple_of(start + i * count, 16), count)
            second = (first[part, :].astype(F32) + ret[part, :].astype(F32)).astype(BF16)
            x[part, :] = second
            first[part, :] = (norm(second.astype(F32)) * gains[2:3, :]).astype(BF16)

        @pl.loop(0, FFH // 256)
        def _(j):
            c = pl.ds(pl.multiple_of(j * 256, 256), 256)
            g = pl.ds(pl.multiple_of(FFH + j * 256, 256), 256)
            value = dot(first[rows, :], win[:, c])
            gate = dot(first[rows, :], win[:, g])
            gelu = 0.5 * gate * (1.0 + lax.erf(gate * (1.0 / math.sqrt(2.0))))
            inner[0:size, c] = (value * gelu).astype(BF16)

        for c0, c1 in ((0, 256), (256, 512), (512, D)):
            result[rows, c0:c1] = (
                x[rows, c0:c1].astype(F32) + dot(inner[0:size, :], wout[:, c0:c1])
            ).astype(BF16)
        for j in range(OWNERS):
            store = pltpu.make_async_copy(
                result.at[pl.ds(start + count * j, count)],
                out.at[pl.ds(BLOCK * j + inside, count)],
                sem_out.at[half * OWNERS + j],
            )
            store.start()
            stores.append(store)

    @pl.loop(1, CLIP)
    def _(d):
        ref_copy(d).wait_send()

    for half in range(2):

        @pl.loop(1, FRAME)
        def _(d):
            @pl.when(is_owner(d))
            def _():
                go_copy(half, d).wait_send()

            @pl.when(me_f < OWNERS)
            def _():
                back_copy(half, d).wait_send()

    for store in stores:
        store.wait()


def time_embedding(steps):
    half = D // 2
    freqs = jnp.exp(-math.log(10000.0) * jnp.arange(half, dtype=F32) / half)
    angles = steps.astype(F32)[:, None] * freqs[None, :]
    return jnp.concatenate([jnp.cos(angles), jnp.sin(angles)], axis=-1).astype(BF16)


def per_device(
    latents, timestep, ref_features, norm_gains, w_spatial, w_temporal, w_time, w_in, w_out
):
    emb = jnp.broadcast_to(time_embedding(timestep), (16, D))
    vmem = pl.BlockSpec(memory_space=pltpu.VMEM)
    hbm = pl.BlockSpec(memory_space=pl.ANY)
    sems = pltpu.SemaphoreType.DMA
    result = pl.pallas_call(
        body,
        out_shape=jax.ShapeDtypeStruct((ROWS, D), BF16),
        in_specs=[hbm, vmem, vmem, vmem, hbm, hbm, hbm, hbm, hbm],
        out_specs=hbm,
        scratch_shapes=[
            pltpu.VMEM((ROWS, D), BF16),
            pltpu.VMEM((ROWS, D), BF16),
            pltpu.VMEM((ROWS, D), BF16),
            pltpu.VMEM((ROWS, WIDE), BF16),
            pltpu.VMEM((WIDE, KEYS_SELF), BF16),
            pltpu.VMEM((KEYS_SELF, WIDE), BF16),
            pltpu.VMEM((REF_PAD, D), BF16),
            pltpu.VMEM((KEYS_REF, D), BF16),
            pltpu.VMEM((WIDE, KEYS_REF), BF16),
            pltpu.VMEM((KEYS_REF, WIDE), BF16),
            pltpu.VMEM((ROWS, WIDE), F32),
            pltpu.VMEM((448, WIDE), BF16),
            pltpu.VMEM((D, WIDE), BF16),
            pltpu.VMEM((D, WIDE), BF16),
            pltpu.VMEM((D, WIDE), BF16),
            pltpu.VMEM((WIDE, D), BF16),
            pltpu.VMEM((4, D, D), BF16),
            pltpu.VMEM((4, D, D), BF16),
            pltpu.VMEM((D, 2 * D), BF16),
            pltpu.VMEM((D, 2 * FFH), BF16),
            pltpu.VMEM((FFH, D), BF16),
            pltpu.VMEM((16, 2 * D), F32),
            pltpu.VMEM((FRAME, PAD, D), BF16),
            pltpu.VMEM((FRAME, D, PAD), BF16),
            pltpu.VMEM((FRAME, 64, D), BF16),
            pltpu.VMEM((FRAME, 48, D), BF16),
            pltpu.VMEM((512, D), BF16),
            pltpu.VMEM((512, D), BF16),
            pltpu.VMEM((512, D), BF16),
            pltpu.VMEM((512, D), BF16),
            pltpu.VMEM((FRAME, 64, D), BF16),
            pltpu.VMEM((FRAME, 48, D), BF16),
            pltpu.VMEM((ROWS, D), BF16),
            pltpu.VMEM((448, FFH), BF16),
            pltpu.VMEM((ROWS, D), BF16),
            sems((2 * OWNERS,)),
            sems((5,)),
            sems((2 * OWNERS,)),
            sems((CLIP,)),
            sems((CLIP,)),
            sems((2 * FRAME,)),
            sems((2 * FRAME,)),
            sems((2 * FRAME,)),
            sems((2 * FRAME,)),
        ],
        compiler_params=pltpu.CompilerParams(
            collective_id=0, has_side_effects=True, vmem_limit_bytes=60 * 1024 * 1024
        ),
        name="block",
    )(latents[0], ref_features, emb, norm_gains, w_spatial, w_temporal, w_time, w_in, w_out)
    return result[None]


def solution(mesh):
    placed = (
        P(("clip", "frame"), None, None),
        P(("clip", "frame")),
        P("clip", None),
        P(),
        P(),
        P(),
        P(),
        P(),
        P(),
    )
    return jax.shard_map(
        per_device,
        mesh=mesh,
        in_specs=placed,
        out_specs=P(("clip", "frame"), None, None),
        check_vma=False,
    )
```

```python
import math

import jax
import jax.numpy as jnp
from jax import lax
from jax.experimental import pallas as pl
from jax.experimental.pallas import tpu as pltpu
from jax.sharding import PartitionSpec as P

HEADS = 8
HEAD = 80
D = 640
FFH = 2560
ROWS = 784
PAD = 128
WIDE = HEADS * PAD
CLIP = 16
FRAME = 8
OWNERS = 7
BLOCK = 112
REF = 49
REF_PAD = 64
KEYS_SELF = 768
KEYS_REF = CLIP * REF_PAD
HALVES = ((0, 64, 0), (448, 48, 64))
LOG2E = 1.4426950408889634
FACTOR = LOG2E / math.sqrt(HEAD)
F32 = jnp.float32
BF16 = jnp.bfloat16
MESH = pl.DeviceIdType.MESH


def dot(a, b):
    return jnp.dot(a, b, preferred_element_type=F32)


def norm(wide):
    mean = jnp.mean(wide, axis=-1, keepdims=True)
    centered = wide - mean
    variance = jnp.mean(centered * centered, axis=-1, keepdims=True)
    return centered * lax.rsqrt(variance + 1e-05)


def iota(shape, axis):
    return lax.broadcasted_iota(jnp.int32, shape, axis)


def head_of(column):
    return (column * 52429) >> 22


def attend(rows, size, keys, q, k_t, v, held, floor, finish):
    def scores(n):
        c = pl.ds(n * PAD, PAD)
        s = dot(q[rows, c], k_t[c, :])
        held[n % 2, 0:size, 0:keys] = s
        top = jnp.max(s, axis=1, keepdims=True)
        return top if floor is None else jnp.maximum(top, floor(c))

    top = scores(0)
    for n in range(HEADS):
        c = pl.ds(n * PAD, PAD)
        later = scores(n + 1) if n + 1 < HEADS else None
        weights = jnp.exp2(held[n % 2, 0:size, 0:keys] - top).astype(BF16)
        finish(c, top, dot(weights, v[:, c]))
        top = later


def body(
    lat, ref, emb, gains, w_spatial, w_temporal, w_time, w_in, w_out, out,
    x, first, h, q, k_t, v, ref_stage, ref_all, kr_t, vr, acc, held, attn, wq, wk, wv, wo,
    ws, wt, wtime, win, wout, mod, spread, gather,
    recv_a, recv_b, moved_a, moved_b, ret, inner,
    sem_x, sem_w, sem_out, ref_send, ref_recv, go_send, go_recv, back_send, back_recv,
):
    swap = ws.at[0]
    wtp = (ws.at[1], ws.at[2], ws.at[3], wt.at[0])
    tq, tk, tv, mixed = (w.at[0:512, 0:D] for w in (wq, wk, wv, wtime))
    result = ret

    me_c = lax.axis_index("clip")
    me_f = lax.axis_index("frame")

    loads_x = []
    for half, (start, count, inside) in enumerate(HALVES):
        for j in range(OWNERS):
            loads_x.append(
                pltpu.make_async_copy(
                    lat.at[pl.ds(BLOCK * j + inside, count)],
                    x.at[pl.ds(start + count * j, count)],
                    sem_x.at[half * OWNERS + j],
                )
            )
    loads_ws = [pltpu.make_async_copy(w_spatial.at[i], ws.at[i], sem_w.at[4 + i]) for i in range(4)]
    load_wtime = pltpu.make_async_copy(w_time, wtime, sem_w.at[0])
    load_wt = pltpu.make_async_copy(w_temporal, wt, sem_w.at[1])
    load_win = pltpu.make_async_copy(w_in, win, sem_w.at[2])
    load_wout = pltpu.make_async_copy(w_out, wout, sem_w.at[3])
    for load in loads_x:
        load.start()
    for load in loads_ws:
        load.start()

    ref_stage[...] = jnp.zeros_like(ref_stage)
    ref_stage[0:REF, :] = ref[...]

    barrier = pltpu.get_barrier_semaphore()

    @pl.loop(1, CLIP)
    def _(d):
        pl.semaphore_signal(
            barrier, inc=1, device_id={"clip": lax.rem(me_c + d, CLIP)}, device_id_type=MESH
        )

    @pl.loop(1, FRAME)
    def _(d):
        pl.semaphore_signal(
            barrier, inc=1, device_id={"frame": lax.rem(me_f + d, FRAME)}, device_id_type=MESH
        )

    pl.semaphore_wait(barrier, CLIP + FRAME - 2)

    def ref_copy(d):
        return pltpu.make_async_remote_copy(
            src_ref=ref_stage,
            dst_ref=ref_all.at[pl.ds(pl.multiple_of(me_c * REF_PAD, REF_PAD), REF_PAD)],
            send_sem=ref_send.at[d],
            recv_sem=ref_recv.at[d],
            device_id={"clip": lax.rem(me_c + d, CLIP)},
            device_id_type=MESH,
        )

    @pl.loop(1, CLIP)
    def _(d):
        ref_copy(d).start()

    ref_all[pl.ds(pl.multiple_of(me_c * REF_PAD, REF_PAD), REF_PAD), :] = ref_stage[...]

    wq[...] = jnp.zeros_like(wq)
    wk[...] = jnp.zeros_like(wk)
    wv[...] = jnp.zeros_like(wv)
    wo[...] = jnp.zeros_like(wo)

    for load in loads_x:
        load.wait()

    @pl.loop(0, ROWS // BLOCK)
    def _(i):
        rows = pl.ds(pl.multiple_of(i * BLOCK, BLOCK), BLOCK)
        h[rows, :] = (norm(x[rows, :].astype(F32)) * gains[0:1, :]).astype(BF16)

    for i, target in enumerate((wq, wk, wv)):
        loads_ws[i].wait()
        for n in range(HEADS):
            target[:, PAD * n : PAD * n + HEAD] = ws[i, :, HEAD * n : HEAD * n + HEAD]
    loads_ws[3].wait()
    for n in range(HEADS):
        wo[PAD * n : PAD * n + HEAD, :] = ws[3, HEAD * n : HEAD * n + HEAD, :]
    load_wtime.start()
    load_wt.start()
    load_win.start()
    load_wout.start()

    for j in range(WIDE // 256):
        c = pl.ds(j * 256, 256)
        lane = iota((1, 256), 1) & (PAD - 1)
        q[:, c] = jnp.where(lane == HEAD, 1.0, dot(h[...], wq[:, c]) * FACTOR).astype(BF16)
        k_t[c, :] = dot(h[0:KEYS_SELF, :], wk[:, c]).astype(BF16).T
        v[:, c] = jnp.where(lane == HEAD, 1.0, dot(h[0:KEYS_SELF, :], wv[:, c])).astype(BF16)

    def own(c, top, o):
        acc[:, c] = jnp.where(iota((1, PAD), 1) == HEAD + 1, top, o)

    attend(pl.ds(0, ROWS), ROWS, KEYS_SELF, q, k_t, v, held, None, own)

    load_wtime.wait()
    mod[...] = dot(emb[...], wtime[...])

    load_wt.wait()
    column = iota((D, D), 1)
    source = HEAD * ((column & (PAD - 1)) >> 4) + 16 * (column >> 7) + (column & 15)
    swap[...] = (iota((D, D), 0) == source).astype(F32).astype(BF16)
    for i in range(3):
        for c0, c1 in ((0, 256), (256, 512), (512, D)):
            wtp[i][:, c0:c1] = dot(wt[i], swap[:, c0:c1]).astype(BF16)
    for n in range(HEADS):
        for r in range(D // PAD):
            wtp[3][PAD * r + 16 * n : PAD * r + 16 * n + 16, :] = wt[
                3, HEAD * n + 16 * r : HEAD * n + 16 * r + 16, :
            ]
    place = iota((FRAME * PAD, PAD), 0)
    pair = FRAME * (place >> 7) + ((place & (PAD - 1)) >> 4)
    gather[...] = ((iota((FRAME * PAD, PAD), 1) & 63) == pair).astype(F32).astype(BF16)
    place = iota((PAD, FRAME * PAD), 1)
    pair = FRAME * (place >> 7) + ((place & (PAD - 1)) >> 4)
    spread[...] = (iota((PAD, FRAME * PAD), 0) == pair).astype(F32).astype(BF16)

    @pl.loop(1, CLIP)
    def _(d):
        ref_copy(d).wait_recv()

    row = iota((PAD, 16), 0)
    tail = iota((PAD, 16), 1)
    place = ((row < REF_PAD) & (row == tail + REF)) | ((row == REF_PAD + REF) & (tail == 15))
    placed = dot(place.astype(F32).astype(BF16), h[KEYS_SELF:ROWS, :])
    ref_all[0:PAD, :] = (ref_all[0:PAD, :].astype(F32) + placed).astype(BF16)

    for j in range(WIDE // 256):
        c = pl.ds(j * 256, 256)
        lane = iota((1, 256), 1) & (PAD - 1)
        key = iota((KEYS_REF, 1), 0)
        valid = ((key & (REF_PAD - 1)) < REF) | (key < REF_PAD) | (key == REF_PAD + REF)
        mask = jnp.where(valid, 0.0, -1e30)
        kr_t[c, :] = jnp.where(lane == HEAD, mask, dot(ref_all[...], wk[:, c])).astype(BF16).T
        vr[:, c] = jnp.where(lane == HEAD, 1.0, dot(ref_all[...], wv[:, c])).astype(BF16)

    def go_copy(half, d):
        start, count, _ = HALVES[half]
        target = lax.rem(me_f + d, FRAME)
        block = lax.min(target, OWNERS - 1)
        return pltpu.make_async_remote_copy(
            src_ref=h.at[pl.ds(pl.multiple_of(start + block * count, 16), count)],
            dst_ref=(recv_a, recv_b)[half].at[me_f],
            send_sem=go_send.at[half * FRAME + d],
            recv_sem=go_recv.at[half * FRAME + d],
            device_id={"frame": target},
            device_id_type=MESH,
        )

    def is_owner(d):
        return lax.rem(me_f + d, FRAME) < OWNERS

    def comes_from_owner(d):
        return lax.rem(me_f + FRAME - d, FRAME) < OWNERS

    for half, (start, count, _) in enumerate(HALVES):
        size = count * OWNERS
        rows = pl.ds(start, size)

        def own_top(c):
            return acc[rows, c][:, HEAD + 1 : HEAD + 2]

        def merge(c, top, o):
            before = acc[rows, c]
            o = o + before * jnp.exp2(before[:, HEAD + 1 : HEAD + 2] - top)
            attn[0:size, c] = (o * (1.0 / o[:, HEAD : HEAD + 1])).astype(BF16)

        attend(rows, size, KEYS_REF, q, kr_t, vr, held, own_top, merge)

        for c0, c1 in ((0, 256), (256, 512), (512, D)):
            first[rows, c0:c1] = (
                x[rows, c0:c1].astype(F32) + dot(attn[0:size, :], wo[:, c0:c1])
            ).astype(BF16)

        @pl.loop(0, OWNERS)
        def _(i):
            part = pl.ds(pl.multiple_of(start + i * count, 16), count)
            normed = norm(first[part, :].astype(F32)) * gains[1:2, :]
            h[part, :] = (normed * (1.0 + mod[0:1, D:]) + mod[0:1, :D]).astype(BF16)

        @pl.loop(1, FRAME)
        def _(d):
            @pl.when(is_owner(d))
            def _():
                go_copy(half, d).start()

        @pl.when(me_f < OWNERS)
        def _():
            (recv_a, recv_b)[half][me_f] = h[
                pl.ds(pl.multiple_of(start + lax.min(me_f, OWNERS - 1) * count, 16), count), :
            ]

    def back_copy(half, d):
        start, count, _ = HALVES[half]
        target = lax.rem(me_f + d, FRAME)
        return pltpu.make_async_remote_copy(
            src_ref=(moved_a, moved_b)[half].at[target],
            dst_ref=ret.at[pl.ds(pl.multiple_of(start + lax.min(me_f, OWNERS - 1) * count, 16), count)],
            send_sem=back_send.at[half * FRAME + d],
            recv_sem=back_recv.at[half * FRAME + d],
            device_id={"frame": target},
            device_id_type=MESH,
        )

    @pl.when(me_f < OWNERS)
    def _():
        for half, (start, count, _) in enumerate(HALVES):
            size = count * FRAME
            recv = (recv_a, recv_b)[half]
            moved = (moved_a, moved_b)[half]

            @pl.loop(1, FRAME)
            def _(d):
                go_copy(half, d).wait_recv()

            for c0, c1 in ((0, 256), (256, 512), (512, D)):
                states = recv[...].reshape(size, D)
                tq[0:size, c0:c1] = (dot(states, wtp[0][:, c0:c1]) * FACTOR).astype(BF16)
                tk[0:size, c0:c1] = dot(states, wtp[1][:, c0:c1]).astype(BF16)
                tv[0:size, c0:c1] = dot(states, wtp[2][:, c0:c1]).astype(BF16)

            for f in range(FRAME):
                queries = tq[f * count : (f + 1) * count, :].astype(F32)
                for g in range(FRAME):
                    pairs = queries * tk[g * count : (g + 1) * count, :].astype(F32)
                    part = pairs[:, 0:PAD]
                    for r in range(1, D // PAD):
                        part = part + pairs[:, PAD * r : PAD * r + PAD]
                    attn[f * count : (f + 1) * count, PAD * g : PAD * g + PAD] = part.astype(BF16)
            s = dot(attn[0:size, :], gather[...])
            top = s
            for shift in (8, 16, 32):
                top = jnp.maximum(top, pltpu.roll(top, shift, 1))
            e = jnp.exp2(s - top)
            total = e
            for shift in (8, 16, 32):
                total = total + pltpu.roll(total, shift, 1)
            weights = (e / total).astype(BF16)
            for c0 in range(0, FRAME * PAD, 256):
                held[0, 0:size, c0 : c0 + 256] = dot(weights, spread[:, c0 : c0 + 256])
            for f in range(FRAME):
                own_rows = slice(f * count, (f + 1) * count)
                for r in range(D // PAD):
                    c = slice(PAD * r, PAD * r + PAD)
                    sums = None
                    for g in range(FRAME):
                        term = held[0, own_rows, PAD * g : PAD * g + PAD] * tv[
                            g * count : (g + 1) * count, c
                        ].astype(F32)
                        sums = term if sums is None else sums + term
                    mixed[own_rows, c] = sums.astype(BF16)
            for c0, c1 in ((0, 256), (256, 512), (512, D)):
                moved[:, :, c0:c1] = (
                    dot(mixed[0:size, :], wtp[3][:, c0:c1]).astype(BF16).reshape(FRAME, count, c1 - c0)
                )

            @pl.loop(1, FRAME)
            def _(d):
                back_copy(half, d).start()

            ret[pl.ds(pl.multiple_of(start + lax.min(me_f, OWNERS - 1) * count, 16), count), :] = moved[
                me_f
            ]

    load_win.wait()
    load_wout.wait()
    stores = []
    for half, (start, count, inside) in enumerate(HALVES):
        size = count * OWNERS
        rows = pl.ds(start, size)

        @pl.loop(1, FRAME)
        def _(d):
            @pl.when(comes_from_owner(d))
            def _():
                back_copy(half, d).wait_recv()

        @pl.loop(0, OWNERS)
        def _(i):
            part = pl.ds(pl.multiple_of(start + i * count, 16), count)
            second = (first[part, :].astype(F32) + ret[part, :].astype(F32)).astype(BF16)
            x[part, :] = second
            first[part, :] = (norm(second.astype(F32)) * gains[2:3, :]).astype(BF16)

        def halves(j):
            states = first[rows, :]
            return (
                dot(states, win[:, 256 * j : 256 * j + 256]),
                dot(states, win[:, FFH + 256 * j : FFH + 256 * j + 256]),
            )

        now = halves(0)
        for j in range(FFH // 256):
            later = halves(j + 1) if j + 1 < FFH // 256 else None
            value, gate = now
            gelu = 0.5 * gate * (1.0 + lax.erf(gate * (1.0 / math.sqrt(2.0))))
            inner[0:size, 256 * j : 256 * j + 256] = (value * gelu).astype(BF16)
            now = later

        for c0, c1 in ((0, 256), (256, 512), (512, D)):
            result[rows, c0:c1] = (
                x[rows, c0:c1].astype(F32) + dot(inner[0:size, :], wout[:, c0:c1])
            ).astype(BF16)
        for j in range(OWNERS):
            store = pltpu.make_async_copy(
                result.at[pl.ds(start + count * j, count)],
                out.at[pl.ds(BLOCK * j + inside, count)],
                sem_out.at[half * OWNERS + j],
            )
            store.start()
            stores.append(store)

    @pl.loop(1, CLIP)
    def _(d):
        ref_copy(d).wait_send()

    for half in range(2):

        @pl.loop(1, FRAME)
        def _(d):
            @pl.when(is_owner(d))
            def _():
                go_copy(half, d).wait_send()

            @pl.when(me_f < OWNERS)
            def _():
                back_copy(half, d).wait_send()

    for store in stores:
        store.wait()


def time_embedding(steps):
    half = D // 2
    freqs = jnp.exp(-math.log(10000.0) * jnp.arange(half, dtype=F32) / half)
    angles = steps.astype(F32)[:, None] * freqs[None, :]
    return jnp.concatenate([jnp.cos(angles), jnp.sin(angles)], axis=-1).astype(BF16)


def per_device(
    latents, timestep, ref_features, norm_gains, w_spatial, w_temporal, w_time, w_in, w_out
):
    emb = jnp.broadcast_to(time_embedding(timestep), (16, D))
    vmem = pl.BlockSpec(memory_space=pltpu.VMEM)
    hbm = pl.BlockSpec(memory_space=pl.ANY)
    sems = pltpu.SemaphoreType.DMA
    result = pl.pallas_call(
        body,
        out_shape=jax.ShapeDtypeStruct((ROWS, D), BF16),
        in_specs=[hbm, vmem, vmem, vmem, hbm, hbm, hbm, hbm, hbm],
        out_specs=hbm,
        scratch_shapes=[
            pltpu.VMEM((ROWS, D), BF16),
            pltpu.VMEM((ROWS, D), BF16),
            pltpu.VMEM((ROWS, D), BF16),
            pltpu.VMEM((ROWS, WIDE), BF16),
            pltpu.VMEM((WIDE, KEYS_SELF), BF16),
            pltpu.VMEM((KEYS_SELF, WIDE), BF16),
            pltpu.VMEM((REF_PAD, D), BF16),
            pltpu.VMEM((KEYS_REF, D), BF16),
            pltpu.VMEM((WIDE, KEYS_REF), BF16),
            pltpu.VMEM((KEYS_REF, WIDE), BF16),
            pltpu.VMEM((ROWS, WIDE), F32),
            pltpu.VMEM((2, ROWS, KEYS_REF), F32),
            pltpu.VMEM((512, WIDE), BF16),
            pltpu.VMEM((D, WIDE), BF16),
            pltpu.VMEM((D, WIDE), BF16),
            pltpu.VMEM((D, WIDE), BF16),
            pltpu.VMEM((WIDE, D), BF16),
            pltpu.VMEM((4, D, D), BF16),
            pltpu.VMEM((4, D, D), BF16),
            pltpu.VMEM((D, 2 * D), BF16),
            pltpu.VMEM((D, 2 * FFH), BF16),
            pltpu.VMEM((FFH, D), BF16),
            pltpu.VMEM((16, 2 * D), F32),
            pltpu.VMEM((PAD, FRAME * PAD), BF16),
            pltpu.VMEM((FRAME * PAD, PAD), BF16),
            pltpu.VMEM((FRAME, 64, D), BF16),
            pltpu.VMEM((FRAME, 48, D), BF16),
            pltpu.VMEM((FRAME, 64, D), BF16),
            pltpu.VMEM((FRAME, 48, D), BF16),
            pltpu.VMEM((ROWS, D), BF16),
            pltpu.VMEM((448, FFH), BF16),
            sems((2 * OWNERS,)),
            sems((8,)),
            sems((2 * OWNERS,)),
            sems((CLIP,)),
            sems((CLIP,)),
            sems((2 * FRAME,)),
            sems((2 * FRAME,)),
            sems((2 * FRAME,)),
            sems((2 * FRAME,)),
        ],
        compiler_params=pltpu.CompilerParams(
            collective_id=0, has_side_effects=True, vmem_limit_bytes=60 * 1024 * 1024
        ),
        name="block",
    )(latents[0], ref_features, emb, norm_gains, w_spatial, w_temporal, w_time, w_in, w_out)
    return result[None]


def solution(mesh):
    placed = (
        P(("clip", "frame"), None, None),
        P(("clip", "frame")),
        P("clip", None),
        P(),
        P(),
        P(),
        P(),
        P(),
        P(),
    )
    return jax.shard_map(
        per_device,
        mesh=mesh,
        in_specs=placed,
        out_specs=P(("clip", "frame"), None, None),
        check_vma=False,
    )
```

```python
import math

import jax
import jax.numpy as jnp
from jax import lax
from jax.experimental import pallas as pl
from jax.experimental.pallas import tpu as pltpu
from jax.sharding import PartitionSpec as P

HEADS = 8
HEAD = 80
D = 640
FFH = 2560
ROWS = 784
PAD = 128
WIDE = HEADS * PAD
CLIP = 16
FRAME = 8
OWNERS = 7
BLOCK = 112
REF = 49
REF_PAD = 64
KEYS_SELF = 768
KEYS_REF = CLIP * REF_PAD
HALVES = ((0, 64, 0), (448, 48, 64))
LOG2E = 1.4426950408889634
FACTOR = LOG2E / math.sqrt(HEAD)
F32 = jnp.float32
BF16 = jnp.bfloat16
MESH = pl.DeviceIdType.MESH


def dot(a, b):
    return jnp.dot(a, b, preferred_element_type=F32)


def norm(wide):
    mean = jnp.mean(wide, axis=-1, keepdims=True)
    centered = wide - mean
    variance = jnp.mean(centered * centered, axis=-1, keepdims=True)
    return centered * lax.rsqrt(variance + 1e-05)


def iota(shape, axis):
    return lax.broadcasted_iota(jnp.int32, shape, axis)


def head_of(column):
    return (column * 52429) >> 22


def attend(rows, size, keys, q, k_t, v, held, floor, finish, per):
    def columns(n):
        return pl.ds(pl.multiple_of(n * PAD, PAD), PAD)

    def scores(n, slot):
        c = columns(n)
        s = dot(q[rows, c], k_t[c, :])
        held[slot, 0:size, 0:keys] = s
        top = jnp.max(s, axis=1, keepdims=True)
        return top if floor is None else jnp.maximum(top, floor(c))

    @pl.loop(0, HEADS // per)
    def _(i):
        top = scores(i * per, 0)
        for n in range(per):
            c = columns(i * per + n)
            later = scores(i * per + n + 1, (n + 1) % 2) if n + 1 < per else None
            weights = jnp.exp2(held[n % 2, 0:size, 0:keys] - top).astype(BF16)
            finish(c, top, dot(weights, v[:, c]))
            top = later


def body(
    lat, ref, emb, gains, w_spatial, w_temporal, w_time, w_in, w_out, out,
    x, first, h, q, k_t, v, ref_stage, ref_all, kr_t, vr, acc, held, attn, wq, wk, wv, wo,
    ws, wt, wtime, win, wout, mod, spread, gather,
    recv_a, recv_b, moved_a, moved_b, ret, inner,
    sem_x, sem_w, sem_out, ref_send, ref_recv, go_send, go_recv, back_send, back_recv,
):
    swap = ws.at[0]
    wtp = (ws.at[1], ws.at[2], ws.at[3], wt.at[0])
    tq, tk, tv, mixed = (w.at[0:512, 0:D] for w in (wq, wk, wv, wtime))
    result = ret

    me_c = lax.axis_index("clip")
    me_f = lax.axis_index("frame")

    loads_x = []
    for half, (start, count, inside) in enumerate(HALVES):
        for j in range(OWNERS):
            loads_x.append(
                pltpu.make_async_copy(
                    lat.at[pl.ds(BLOCK * j + inside, count)],
                    x.at[pl.ds(start + count * j, count)],
                    sem_x.at[half * OWNERS + j],
                )
            )
    loads_ws = [pltpu.make_async_copy(w_spatial.at[i], ws.at[i], sem_w.at[4 + i]) for i in range(4)]
    load_wtime = pltpu.make_async_copy(w_time, wtime, sem_w.at[0])
    load_wt = pltpu.make_async_copy(w_temporal, wt, sem_w.at[1])
    load_win = pltpu.make_async_copy(w_in, win, sem_w.at[2])
    load_wout = pltpu.make_async_copy(w_out, wout, sem_w.at[3])
    for load in loads_x:
        load.start()
    for load in loads_ws:
        load.start()

    ref_stage[...] = jnp.zeros_like(ref_stage)
    ref_stage[0:REF, :] = ref[...]

    z_hi, y, core = lax.div(me_c, 8), lax.rem(lax.div(me_c, 2), 4), lax.rem(me_c, 2)
    other_frame = me_f + 1 - 2 * lax.rem(me_f, 2)
    sibling = me_c + 1 - 2 * core
    routes = [(0, dy) for dy in (1, 2, 3)] + [(1, dy) for dy in range(4)]

    def clip_of(far, dy, at_core):
        half = (1 - z_hi) if far else z_hi
        return half * 8 + lax.rem(y + dy, 4) * 2 + at_core

    targets = [(clip_of(far, dy, core), other_frame if far else me_f) for far, dy in routes]
    targets.append((sibling, me_f))
    barrier = pltpu.get_barrier_semaphore()
    for clip, frame in targets:
        pl.semaphore_signal(
            barrier, inc=1, device_id={"clip": clip, "frame": frame}, device_id_type=MESH
        )

    @pl.loop(1, FRAME)
    def _(d):
        pl.semaphore_signal(
            barrier,
            inc=1,
            device_id={"clip": me_c, "frame": lax.rem(me_f + d, FRAME)},
            device_id_type=MESH,
        )

    pl.semaphore_wait(barrier, len(targets) + FRAME - 1)

    def ref_rows(clip):
        return ref_all.at[pl.ds(pl.multiple_of(clip * REF_PAD, REF_PAD), REF_PAD)]

    def ref_copy(slot):
        clip, frame = targets[slot]
        return pltpu.make_async_remote_copy(
            src_ref=ref_stage,
            dst_ref=ref_rows(me_c),
            send_sem=ref_send.at[slot],
            recv_sem=ref_recv.at[slot],
            device_id={"clip": clip, "frame": frame},
            device_id_type=MESH,
        )

    def ref_forward(slot):
        far, dy = routes[slot]
        piece = ref_rows(clip_of(far, 4 - dy, core))
        return pltpu.make_async_remote_copy(
            src_ref=piece,
            dst_ref=piece,
            send_sem=ref_send.at[8 + slot],
            recv_sem=ref_recv.at[8 + slot],
            device_id={"clip": sibling, "frame": me_f},
            device_id_type=MESH,
        )

    for slot in range(8):
        ref_copy(slot).start()

    ref_all[pl.ds(pl.multiple_of(me_c * REF_PAD, REF_PAD), REF_PAD), :] = ref_stage[...]

    wq[...] = jnp.zeros_like(wq)
    wk[...] = jnp.zeros_like(wk)
    wv[...] = jnp.zeros_like(wv)
    wo[...] = jnp.zeros_like(wo)

    for load in loads_x:
        load.wait()

    @pl.loop(0, ROWS // BLOCK)
    def _(i):
        rows = pl.ds(pl.multiple_of(i * BLOCK, BLOCK), BLOCK)
        h[rows, :] = (norm(x[rows, :].astype(F32)) * gains[0:1, :]).astype(BF16)

    for i, target in enumerate((wq, wk, wv)):
        loads_ws[i].wait()
        for n in range(HEADS):
            target[:, PAD * n : PAD * n + HEAD] = ws[i, :, HEAD * n : HEAD * n + HEAD]
    loads_ws[3].wait()
    for n in range(HEADS):
        wo[PAD * n : PAD * n + HEAD, :] = ws[3, HEAD * n : HEAD * n + HEAD, :]
    load_wtime.start()
    load_wt.start()
    load_win.start()
    load_wout.start()

    for j in range(WIDE // 256):
        c = pl.ds(j * 256, 256)
        lane = iota((1, 256), 1) & (PAD - 1)
        q[:, c] = jnp.where(lane == HEAD, 1.0, dot(h[...], wq[:, c]) * FACTOR).astype(BF16)
        k_t[c, :] = dot(h[0:KEYS_SELF, :], wk[:, c]).astype(BF16).T
        v[:, c] = jnp.where(lane == HEAD, 1.0, dot(h[0:KEYS_SELF, :], wv[:, c])).astype(BF16)

    def own(c, top, o):
        acc[:, c] = jnp.where(iota((1, PAD), 1) == HEAD + 1, top, o)

    attend(pl.ds(0, ROWS), ROWS, KEYS_SELF, q, k_t, v, held, None, own, 4)

    for slot in range(7):
        ref_copy(slot).wait_recv()
        ref_forward(slot).start()
    load_wtime.wait()
    mod[...] = dot(jnp.broadcast_to(emb[...], (16, D)), wtime[...])

    load_wt.wait()
    column = iota((D, D), 1)
    source = HEAD * ((column & (PAD - 1)) >> 4) + 16 * (column >> 7) + (column & 15)
    swap[...] = (iota((D, D), 0) == source).astype(F32).astype(BF16)
    for i in range(3):
        for c0, c1 in ((0, 256), (256, 512), (512, D)):
            wtp[i][:, c0:c1] = dot(wt[i], swap[:, c0:c1]).astype(BF16)
    for n in range(HEADS):
        for r in range(D // PAD):
            wtp[3][PAD * r + 16 * n : PAD * r + 16 * n + 16, :] = wt[
                3, HEAD * n + 16 * r : HEAD * n + 16 * r + 16, :
            ]
    place = iota((FRAME * PAD, PAD), 0)
    pair = FRAME * (place >> 7) + ((place & (PAD - 1)) >> 4)
    gather[...] = ((iota((FRAME * PAD, PAD), 1) & 63) == pair).astype(F32).astype(BF16)
    place = iota((PAD, FRAME * PAD), 1)
    pair = FRAME * (place >> 7) + ((place & (PAD - 1)) >> 4)
    spread[...] = (iota((PAD, FRAME * PAD), 0) == pair).astype(F32).astype(BF16)

    ref_copy(7).wait_recv()
    for slot in range(7):
        ref_forward(slot).wait()

    row = iota((PAD, 16), 0)
    tail = iota((PAD, 16), 1)
    place = ((row < REF_PAD) & (row == tail + REF)) | ((row == REF_PAD + REF) & (tail == 15))
    placed = dot(place.astype(F32).astype(BF16), h[KEYS_SELF:ROWS, :])
    ref_all[0:PAD, :] = (ref_all[0:PAD, :].astype(F32) + placed).astype(BF16)

    for j in range(WIDE // 256):
        c = pl.ds(j * 256, 256)
        lane = iota((1, 256), 1) & (PAD - 1)
        key = iota((KEYS_REF, 1), 0)
        valid = ((key & (REF_PAD - 1)) < REF) | (key < REF_PAD) | (key == REF_PAD + REF)
        mask = jnp.where(valid, 0.0, -1e30)
        kr_t[c, :] = jnp.where(lane == HEAD, mask, dot(ref_all[...], wk[:, c])).astype(BF16).T
        vr[:, c] = jnp.where(lane == HEAD, 1.0, dot(ref_all[...], wv[:, c])).astype(BF16)

    def go_copy(half, d):
        start, count, _ = HALVES[half]
        target = lax.rem(me_f + d, FRAME)
        block = lax.min(target, OWNERS - 1)
        return pltpu.make_async_remote_copy(
            src_ref=h.at[pl.ds(pl.multiple_of(start + block * count, 16), count)],
            dst_ref=(recv_a, recv_b)[half].at[me_f],
            send_sem=go_send.at[half * FRAME + d],
            recv_sem=go_recv.at[half * FRAME + d],
            device_id={"clip": me_c, "frame": target},
            device_id_type=MESH,
        )

    def is_owner(d):
        return lax.rem(me_f + d, FRAME) < OWNERS

    def comes_from_owner(d):
        return lax.rem(me_f + FRAME - d, FRAME) < OWNERS

    for half, (start, count, _) in enumerate(HALVES):
        size = count * OWNERS
        rows = pl.ds(start, size)

        def own_top(c):
            return acc[rows, c][:, HEAD + 1 : HEAD + 2]

        def merge(c, top, o):
            before = acc[rows, c]
            o = o + before * jnp.exp2(before[:, HEAD + 1 : HEAD + 2] - top)
            attn[0:size, c] = (o * (1.0 / o[:, HEAD : HEAD + 1])).astype(BF16)

        attend(rows, size, KEYS_REF, q, kr_t, vr, held, own_top, merge, 4)

        for c0, c1 in ((0, 256), (256, 512), (512, D)):
            first[rows, c0:c1] = (
                x[rows, c0:c1].astype(F32) + dot(attn[0:size, :], wo[:, c0:c1])
            ).astype(BF16)

        @pl.loop(0, OWNERS)
        def _(i):
            part = pl.ds(pl.multiple_of(start + i * count, 16), count)
            normed = norm(first[part, :].astype(F32)) * gains[1:2, :]
            h[part, :] = (normed * (1.0 + mod[0:1, D:]) + mod[0:1, :D]).astype(BF16)

        @pl.loop(1, FRAME)
        def _(d):
            @pl.when(is_owner(d))
            def _():
                go_copy(half, d).start()

        @pl.when(me_f < OWNERS)
        def _():
            (recv_a, recv_b)[half][me_f] = h[
                pl.ds(pl.multiple_of(start + lax.min(me_f, OWNERS - 1) * count, 16), count), :
            ]

    def back_copy(half, d):
        start, count, _ = HALVES[half]
        target = lax.rem(me_f + d, FRAME)
        return pltpu.make_async_remote_copy(
            src_ref=(moved_a, moved_b)[half].at[target],
            dst_ref=ret.at[pl.ds(pl.multiple_of(start + lax.min(me_f, OWNERS - 1) * count, 16), count)],
            send_sem=back_send.at[half * FRAME + d],
            recv_sem=back_recv.at[half * FRAME + d],
            device_id={"clip": me_c, "frame": target},
            device_id_type=MESH,
        )

    @pl.when(me_f < OWNERS)
    def _():
        for half, (start, count, _) in enumerate(HALVES):
            size = count * FRAME
            recv = (recv_a, recv_b)[half]
            moved = (moved_a, moved_b)[half]

            @pl.loop(1, FRAME)
            def _(d):
                go_copy(half, d).wait_recv()

            for c0, c1 in ((0, 256), (256, 512), (512, D)):
                states = recv[...].reshape(size, D)
                tq[0:size, c0:c1] = (dot(states, wtp[0][:, c0:c1]) * FACTOR).astype(BF16)
                tk[0:size, c0:c1] = dot(states, wtp[1][:, c0:c1]).astype(BF16)
                tv[0:size, c0:c1] = dot(states, wtp[2][:, c0:c1]).astype(BF16)

            @pl.loop(0, FRAME)
            def _(f):
                own_rows = pl.ds(pl.multiple_of(f * count, 16), count)
                queries = tq[own_rows, :].astype(F32)
                for g in range(FRAME):
                    pairs = queries * tk[g * count : (g + 1) * count, :].astype(F32)
                    part = pairs[:, 0:PAD]
                    for r in range(1, D // PAD):
                        part = part + pairs[:, PAD * r : PAD * r + PAD]
                    attn[own_rows, PAD * g : PAD * g + PAD] = part.astype(BF16)

            s = dot(attn[0:size, :], gather[...])
            top = s
            for shift in (8, 16, 32):
                top = jnp.maximum(top, pltpu.roll(top, shift, 1))
            e = jnp.exp2(s - top)
            total = e
            for shift in (8, 16, 32):
                total = total + pltpu.roll(total, shift, 1)
            weights = (e / total).astype(BF16)
            for c0 in range(0, FRAME * PAD, 256):
                held[0, 0:size, c0 : c0 + 256] = dot(weights, spread[:, c0 : c0 + 256])
            @pl.loop(0, FRAME)
            def _(f):
                own_rows = pl.ds(pl.multiple_of(f * count, 16), count)
                for r in range(D // PAD):
                    c = slice(PAD * r, PAD * r + PAD)
                    sums = None
                    for g in range(FRAME):
                        term = held[0, own_rows, PAD * g : PAD * g + PAD] * tv[
                            g * count : (g + 1) * count, c
                        ].astype(F32)
                        sums = term if sums is None else sums + term
                    mixed[own_rows, c] = sums.astype(BF16)

            for c0, c1 in ((0, 256), (256, 512), (512, D)):
                moved[:, :, c0:c1] = (
                    dot(mixed[0:size, :], wtp[3][:, c0:c1]).astype(BF16).reshape(FRAME, count, c1 - c0)
                )

            @pl.loop(1, FRAME)
            def _(d):
                back_copy(half, d).start()

            ret[pl.ds(pl.multiple_of(start + lax.min(me_f, OWNERS - 1) * count, 16), count), :] = moved[
                me_f
            ]

    load_win.wait()
    load_wout.wait()
    stores = []
    for half, (start, count, inside) in enumerate(HALVES):
        size = count * OWNERS
        rows = pl.ds(start, size)

        @pl.loop(1, FRAME)
        def _(d):
            @pl.when(comes_from_owner(d))
            def _():
                back_copy(half, d).wait_recv()

        @pl.loop(0, OWNERS)
        def _(i):
            part = pl.ds(pl.multiple_of(start + i * count, 16), count)
            second = (first[part, :].astype(F32) + ret[part, :].astype(F32)).astype(BF16)
            x[part, :] = second
            first[part, :] = (norm(second.astype(F32)) * gains[2:3, :]).astype(BF16)

        @pl.loop(0, 2)
        def _(i):
            for j in range(FFH // 512):
                c = pl.ds(pl.multiple_of(i * (FFH // 2) + 256 * j, 256), 256)
                g = pl.ds(pl.multiple_of(FFH + i * (FFH // 2) + 256 * j, 256), 256)
                value = dot(first[rows, :], win[:, c])
                gate = dot(first[rows, :], win[:, g])
                gelu = 0.5 * gate * (1.0 + lax.erf(gate * (1.0 / math.sqrt(2.0))))
                inner[0:size, c] = (value * gelu).astype(BF16)

        for c0, c1 in ((0, 256), (256, 512), (512, D)):
            result[rows, c0:c1] = (
                x[rows, c0:c1].astype(F32) + dot(inner[0:size, :], wout[:, c0:c1])
            ).astype(BF16)
        for j in range(OWNERS):
            store = pltpu.make_async_copy(
                result.at[pl.ds(start + count * j, count)],
                out.at[pl.ds(BLOCK * j + inside, count)],
                sem_out.at[half * OWNERS + j],
            )
            store.start()
            stores.append(store)

    for slot in range(8):
        ref_copy(slot).wait_send()

    for half in range(2):

        @pl.loop(1, FRAME)
        def _(d):
            @pl.when(is_owner(d))
            def _():
                go_copy(half, d).wait_send()

            @pl.when(me_f < OWNERS)
            def _():
                back_copy(half, d).wait_send()

    for store in stores:
        store.wait()


def time_embedding(steps):
    half = D // 2
    freqs = jnp.exp(-math.log(10000.0) * jnp.arange(half, dtype=F32) / half)
    angles = steps.astype(F32)[:, None] * freqs[None, :]
    return jnp.concatenate([jnp.cos(angles), jnp.sin(angles)], axis=-1).astype(BF16)


def per_device(
    latents, timestep, ref_features, norm_gains, w_spatial, w_temporal, w_time, w_in, w_out
):
    emb = time_embedding(timestep)
    vmem = pl.BlockSpec(memory_space=pltpu.VMEM)
    hbm = pl.BlockSpec(memory_space=pl.ANY)
    sems = pltpu.SemaphoreType.DMA
    result = pl.pallas_call(
        body,
        out_shape=jax.ShapeDtypeStruct((ROWS, D), BF16),
        in_specs=[hbm, vmem, vmem, vmem, hbm, hbm, hbm, hbm, hbm],
        out_specs=hbm,
        scratch_shapes=[
            pltpu.VMEM((ROWS, D), BF16),
            pltpu.VMEM((ROWS, D), BF16),
            pltpu.VMEM((ROWS, D), BF16),
            pltpu.VMEM((ROWS, WIDE), BF16),
            pltpu.VMEM((WIDE, KEYS_SELF), BF16),
            pltpu.VMEM((KEYS_SELF, WIDE), BF16),
            pltpu.VMEM((REF_PAD, D), BF16),
            pltpu.VMEM((KEYS_REF, D), BF16),
            pltpu.VMEM((WIDE, KEYS_REF), BF16),
            pltpu.VMEM((KEYS_REF, WIDE), BF16),
            pltpu.VMEM((ROWS, WIDE), F32),
            pltpu.VMEM((2, ROWS, KEYS_REF), F32),
            pltpu.VMEM((512, WIDE), BF16),
            pltpu.VMEM((D, WIDE), BF16),
            pltpu.VMEM((D, WIDE), BF16),
            pltpu.VMEM((D, WIDE), BF16),
            pltpu.VMEM((WIDE, D), BF16),
            pltpu.VMEM((4, D, D), BF16),
            pltpu.VMEM((4, D, D), BF16),
            pltpu.VMEM((D, 2 * D), BF16),
            pltpu.VMEM((D, 2 * FFH), BF16),
            pltpu.VMEM((FFH, D), BF16),
            pltpu.VMEM((16, 2 * D), F32),
            pltpu.VMEM((PAD, FRAME * PAD), BF16),
            pltpu.VMEM((FRAME * PAD, PAD), BF16),
            pltpu.VMEM((FRAME, 64, D), BF16),
            pltpu.VMEM((FRAME, 48, D), BF16),
            pltpu.VMEM((FRAME, 64, D), BF16),
            pltpu.VMEM((FRAME, 48, D), BF16),
            pltpu.VMEM((ROWS, D), BF16),
            pltpu.VMEM((448, FFH), BF16),
            sems((2 * OWNERS,)),
            sems((8,)),
            sems((2 * OWNERS,)),
            sems((CLIP,)),
            sems((CLIP,)),
            sems((2 * FRAME,)),
            sems((2 * FRAME,)),
            sems((2 * FRAME,)),
            sems((2 * FRAME,)),
        ],
        compiler_params=pltpu.CompilerParams(
            collective_id=0, has_side_effects=True, vmem_limit_bytes=60 * 1024 * 1024
        ),
        name="block",
    )(latents[0], ref_features, emb, norm_gains, w_spatial, w_temporal, w_time, w_in, w_out)
    return result[None]


def solution(mesh):
    placed = (
        P(("clip", "frame"), None, None),
        P(("clip", "frame")),
        P("clip", None),
        P(),
        P(),
        P(),
        P(),
        P(),
        P(),
    )
    return jax.shard_map(
        per_device,
        mesh=mesh,
        in_specs=placed,
        out_specs=P(("clip", "frame"), None, None),
        check_vma=False,
    )
```

```python
import math

import jax
import jax.numpy as jnp
from jax import lax
from jax.experimental import pallas as pl
from jax.experimental.pallas import tpu as pltpu
from jax.sharding import PartitionSpec as P

HEADS = 8
HEAD = 80
D = 640
FFH = 2560
ROWS = 784
PAD = 128
WIDE = HEADS * PAD
CLIP = 16
FRAME = 8
OWNERS = 7
BLOCK = 112
REF = 49
REF_PAD = 64
KEYS_SELF = 768
KEYS_REF = CLIP * REF_PAD
HALVES = ((0, 64, 0), (448, 48, 64))
LOG2E = 1.4426950408889634
FACTOR = LOG2E / math.sqrt(HEAD)
F32 = jnp.float32
BF16 = jnp.bfloat16
MESH = pl.DeviceIdType.MESH


def dot(a, b):
    return jnp.dot(a, b, preferred_element_type=F32)


def norm(wide):
    mean = jnp.mean(wide, axis=-1, keepdims=True)
    centered = wide - mean
    variance = jnp.mean(centered * centered, axis=-1, keepdims=True)
    return centered * lax.rsqrt(variance + 1e-05)


def iota(shape, axis):
    return lax.broadcasted_iota(jnp.int32, shape, axis)


def head_of(column):
    return (column * 52429) >> 22


def attend(rows, size, keys, q, k_t, v, held, floor, finish, per):
    def columns(n):
        return pl.ds(pl.multiple_of(n * PAD, PAD), PAD)

    def scores(n, slot):
        c = columns(n)
        s = dot(q[rows, c], k_t[c, :])
        held[slot, 0:size, 0:keys] = s
        top = jnp.max(s, axis=1, keepdims=True)
        return top if floor is None else jnp.maximum(top, floor(c))

    @pl.loop(0, HEADS // per)
    def _(i):
        top = scores(i * per, 0)
        for n in range(per):
            c = columns(i * per + n)
            later = scores(i * per + n + 1, (n + 1) % 2) if n + 1 < per else None
            weights = jnp.exp2(held[n % 2, 0:size, 0:keys] - top).astype(BF16)
            finish(c, top, dot(weights, v[:, c]))
            top = later


def body(
    lat, ref, emb, gains, w_spatial, w_temporal, w_time, w_in, w_out, out,
    x, first, h, q, k_t, v, ref_stage, ref_all, kr_t, vr, acc, held, attn, wq, wk, wv, wo,
    ws, wt, wtime, win, wout, mod, spread, gather,
    recv_a, recv_b, moved_a, moved_b, ret, inner,
    sem_x, sem_w, sem_out, ref_send, ref_recv, go_send, go_recv, back_send, back_recv,
):
    swap = ws.at[0]
    wtp = (ws.at[1], ws.at[2], ws.at[3], wt.at[0])
    tq, tk, tv, mixed = (w.at[0:512, 0:D] for w in (wq, wk, wv, wtime))
    result = acc.at[:, 0:D]

    me_c = lax.axis_index("clip")
    me_f = lax.axis_index("frame")

    loads_x = []
    for half, (start, count, inside) in enumerate(HALVES):
        for j in range(OWNERS):
            loads_x.append(
                pltpu.make_async_copy(
                    lat.at[pl.ds(BLOCK * j + inside, count)],
                    x.at[pl.ds(start + count * j, count)],
                    sem_x.at[half * OWNERS + j],
                )
            )
    loads_ws = [pltpu.make_async_copy(w_spatial.at[i], ws.at[i], sem_w.at[4 + i]) for i in range(4)]
    load_wtime = pltpu.make_async_copy(w_time, wtime, sem_w.at[0])
    load_wt = pltpu.make_async_copy(w_temporal, wt, sem_w.at[1])
    load_win = pltpu.make_async_copy(w_in, win, sem_w.at[2])
    load_wout = pltpu.make_async_copy(w_out, wout, sem_w.at[3])
    for load in loads_x:
        load.start()
    for load in loads_ws:
        load.start()

    ref_stage[...] = jnp.zeros_like(ref_stage)
    ref_stage[0:REF, :] = ref[...]

    z_hi, y, core = lax.div(me_c, 8), lax.rem(lax.div(me_c, 2), 4), lax.rem(me_c, 2)
    other_frame = me_f + 1 - 2 * lax.rem(me_f, 2)
    sibling = me_c + 1 - 2 * core
    routes = [(0, dy) for dy in (1, 2, 3)] + [(1, dy) for dy in range(4)]

    def clip_of(far, dy, at_core):
        half = (1 - z_hi) if far else z_hi
        return half * 8 + lax.rem(y + dy, 4) * 2 + at_core

    targets = [(clip_of(far, dy, core), other_frame if far else me_f) for far, dy in routes]
    targets.append((sibling, me_f))
    barrier = pltpu.get_barrier_semaphore()
    for clip, frame in targets:
        pl.semaphore_signal(
            barrier, inc=1, device_id={"clip": clip, "frame": frame}, device_id_type=MESH
        )

    @pl.loop(1, FRAME)
    def _(d):
        pl.semaphore_signal(
            barrier,
            inc=1,
            device_id={"clip": me_c, "frame": lax.rem(me_f + d, FRAME)},
            device_id_type=MESH,
        )

    pl.semaphore_wait(barrier, len(targets) + FRAME - 1)

    def ref_rows(clip):
        return ref_all.at[pl.ds(pl.multiple_of(clip * REF_PAD, REF_PAD), REF_PAD)]

    def ref_copy(slot):
        clip, frame = targets[slot]
        return pltpu.make_async_remote_copy(
            src_ref=ref_stage,
            dst_ref=ref_rows(me_c),
            send_sem=ref_send.at[slot],
            recv_sem=ref_recv.at[slot],
            device_id={"clip": clip, "frame": frame},
            device_id_type=MESH,
        )

    def ref_forward(slot):
        far, dy = routes[slot]
        piece = ref_rows(clip_of(far, 4 - dy, core))
        return pltpu.make_async_remote_copy(
            src_ref=piece,
            dst_ref=piece,
            send_sem=ref_send.at[8 + slot],
            recv_sem=ref_recv.at[8 + slot],
            device_id={"clip": sibling, "frame": me_f},
            device_id_type=MESH,
        )

    for slot in range(8):
        ref_copy(slot).start()

    ref_all[pl.ds(pl.multiple_of(me_c * REF_PAD, REF_PAD), REF_PAD), :] = ref_stage[...]

    wq[...] = jnp.zeros_like(wq)
    wk[...] = jnp.zeros_like(wk)
    wv[...] = jnp.zeros_like(wv)
    wo[...] = jnp.zeros_like(wo)

    for load in loads_x:
        load.wait()

    @pl.loop(0, ROWS // BLOCK)
    def _(i):
        rows = pl.ds(pl.multiple_of(i * BLOCK, BLOCK), BLOCK)
        h[rows, :] = (norm(x[rows, :].astype(F32)) * gains[0:1, :]).astype(BF16)

    for i, target in enumerate((wq, wk, wv)):
        loads_ws[i].wait()
        for n in range(HEADS):
            target[:, PAD * n : PAD * n + HEAD] = ws[i, :, HEAD * n : HEAD * n + HEAD]
    loads_ws[3].wait()
    for n in range(HEADS):
        wo[PAD * n : PAD * n + HEAD, :] = ws[3, HEAD * n : HEAD * n + HEAD, :]
    load_wtime.start()
    load_wt.start()
    load_win.start()
    load_wout.start()

    for j in range(WIDE // 256):
        c = pl.ds(j * 256, 256)
        lane = iota((1, 256), 1) & (PAD - 1)
        q[:, c] = jnp.where(lane == HEAD, 1.0, dot(h[...], wq[:, c]) * FACTOR).astype(BF16)
        k_t[c, :] = dot(h[0:KEYS_SELF, :], wk[:, c]).astype(BF16).T
        v[:, c] = jnp.where(lane == HEAD, 1.0, dot(h[0:KEYS_SELF, :], wv[:, c])).astype(BF16)

    def own(c, top, o):
        acc[:, c] = jnp.where(iota((1, PAD), 1) == HEAD + 1, top, o)

    attend(pl.ds(0, ROWS), ROWS, KEYS_SELF, q, k_t, v, held, None, own, 4)

    for slot in range(7):
        ref_copy(slot).wait_recv()
        ref_forward(slot).start()
    load_wtime.wait()
    mod[...] = dot(jnp.broadcast_to(emb[...], (16, D)), wtime[...])

    load_wt.wait()
    column = iota((D, D), 1)
    source = HEAD * ((column & (PAD - 1)) >> 4) + 16 * (column >> 7) + (column & 15)
    swap[...] = (iota((D, D), 0) == source).astype(F32).astype(BF16)
    for i in range(3):
        for c0, c1 in ((0, 256), (256, 512), (512, D)):
            wtp[i][:, c0:c1] = dot(wt[i], swap[:, c0:c1]).astype(BF16)
    for n in range(HEADS):
        for r in range(D // PAD):
            wtp[3][PAD * r + 16 * n : PAD * r + 16 * n + 16, :] = wt[
                3, HEAD * n + 16 * r : HEAD * n + 16 * r + 16, :
            ]
    place = iota((FRAME * PAD, PAD), 0)
    pair = FRAME * (place >> 7) + ((place & (PAD - 1)) >> 4)
    gather[...] = ((iota((FRAME * PAD, PAD), 1) & 63) == pair).astype(F32).astype(BF16)
    place = iota((PAD, FRAME * PAD), 1)
    pair = FRAME * (place >> 7) + ((place & (PAD - 1)) >> 4)
    spread[...] = (iota((PAD, FRAME * PAD), 0) == pair).astype(F32).astype(BF16)

    ref_copy(7).wait_recv()
    for slot in range(7):
        ref_forward(slot).wait()

    row = iota((PAD, 16), 0)
    tail = iota((PAD, 16), 1)
    place = ((row < REF_PAD) & (row == tail + REF)) | ((row == REF_PAD + REF) & (tail == 15))
    placed = dot(place.astype(F32).astype(BF16), h[KEYS_SELF:ROWS, :])
    ref_all[0:PAD, :] = (ref_all[0:PAD, :].astype(F32) + placed).astype(BF16)

    for j in range(WIDE // 256):
        c = pl.ds(j * 256, 256)
        lane = iota((1, 256), 1) & (PAD - 1)
        key = iota((KEYS_REF, 1), 0)
        valid = ((key & (REF_PAD - 1)) < REF) | (key < REF_PAD) | (key == REF_PAD + REF)
        mask = jnp.where(valid, 0.0, -1e30)
        kr_t[c, :] = jnp.where(lane == HEAD, mask, dot(ref_all[...], wk[:, c])).astype(BF16).T
        vr[:, c] = jnp.where(lane == HEAD, 1.0, dot(ref_all[...], wv[:, c])).astype(BF16)

    def go_copy(half, d):
        start, count, _ = HALVES[half]
        target = lax.rem(me_f + d, FRAME)
        block = lax.min(target, OWNERS - 1)
        return pltpu.make_async_remote_copy(
            src_ref=h.at[pl.ds(pl.multiple_of(start + block * count, 16), count)],
            dst_ref=(recv_a, recv_b)[half].at[me_f],
            send_sem=go_send.at[half * FRAME + d],
            recv_sem=go_recv.at[half * FRAME + d],
            device_id={"clip": me_c, "frame": target},
            device_id_type=MESH,
        )

    def is_owner(d):
        return lax.rem(me_f + d, FRAME) < OWNERS

    def comes_from_owner(d):
        return lax.rem(me_f + FRAME - d, FRAME) < OWNERS

    for half, (start, count, _) in enumerate(HALVES):
        size = count * OWNERS
        rows = pl.ds(start, size)

        def own_top(c):
            return acc[rows, c][:, HEAD + 1 : HEAD + 2]

        def merge(c, top, o):
            before = acc[rows, c]
            o = o + before * jnp.exp2(before[:, HEAD + 1 : HEAD + 2] - top)
            attn[0:size, c] = (o * (1.0 / o[:, HEAD : HEAD + 1])).astype(BF16)

        attend(rows, size, KEYS_REF, q, kr_t, vr, held, own_top, merge, 8)

        for c0, c1 in ((0, 256), (256, 512), (512, D)):
            first[rows, c0:c1] = (
                x[rows, c0:c1].astype(F32) + dot(attn[0:size, :], wo[:, c0:c1])
            ).astype(BF16)

        @pl.loop(0, OWNERS)
        def _(i):
            part = pl.ds(pl.multiple_of(start + i * count, 16), count)
            normed = norm(first[part, :].astype(F32)) * gains[1:2, :]
            h[part, :] = (normed * (1.0 + mod[0:1, D:]) + mod[0:1, :D]).astype(BF16)

        @pl.loop(1, FRAME)
        def _(d):
            @pl.when(is_owner(d))
            def _():
                go_copy(half, d).start()

        @pl.when(me_f < OWNERS)
        def _():
            (recv_a, recv_b)[half][me_f] = h[
                pl.ds(pl.multiple_of(start + lax.min(me_f, OWNERS - 1) * count, 16), count), :
            ]

    def back_copy(half, d):
        start, count, _ = HALVES[half]
        target = lax.rem(me_f + d, FRAME)
        return pltpu.make_async_remote_copy(
            src_ref=(moved_a, moved_b)[half].at[target],
            dst_ref=ret.at[pl.ds(pl.multiple_of(start + lax.min(me_f, OWNERS - 1) * count, 16), count)],
            send_sem=back_send.at[half * FRAME + d],
            recv_sem=back_recv.at[half * FRAME + d],
            device_id={"clip": me_c, "frame": target},
            device_id_type=MESH,
        )

    @pl.when(me_f < OWNERS)
    def _():
        for half, (start, count, _) in enumerate(HALVES):
            size = count * FRAME
            recv = (recv_a, recv_b)[half]
            moved = (moved_a, moved_b)[half]

            @pl.loop(1, FRAME)
            def _(d):
                go_copy(half, d).wait_recv()

            for c0, c1 in ((0, 256), (256, 512), (512, D)):
                states = recv[...].reshape(size, D)
                tq[0:size, c0:c1] = (dot(states, wtp[0][:, c0:c1]) * FACTOR).astype(BF16)
                tk[0:size, c0:c1] = dot(states, wtp[1][:, c0:c1]).astype(BF16)
                tv[0:size, c0:c1] = dot(states, wtp[2][:, c0:c1]).astype(BF16)

            def at(f, i):
                return pl.ds(pl.multiple_of(f * count + 16 * i, 16), 16)

            @pl.loop(0, count // 16)
            def _(i):
                for f in range(FRAME):
                    queries = tq[at(f, i), :]
                    for g in range(FRAME):
                        pairs = queries * tk[at(g, i), :]
                        part = pairs[:, 0:PAD]
                        for r in range(1, D // PAD):
                            part = part + pairs[:, PAD * r : PAD * r + PAD]
                        attn[at(f, i), PAD * g : PAD * g + PAD] = part

            s = dot(attn[0:size, :], gather[...])
            top = s
            for shift in (8, 16, 32):
                top = jnp.maximum(top, pltpu.roll(top, shift, 1))
            e = jnp.exp2(s - top)
            total = e
            for shift in (8, 16, 32):
                total = total + pltpu.roll(total, shift, 1)
            weights = (e / total).astype(BF16)
            for c0 in range(0, FRAME * PAD, 256):
                attn[0:size, c0 : c0 + 256] = dot(weights, spread[:, c0 : c0 + 256]).astype(BF16)

            @pl.loop(0, count // 16)
            def _(i):
                for f in range(FRAME):
                    for r in range(D // PAD):
                        c = slice(PAD * r, PAD * r + PAD)
                        terms = [
                            attn[at(f, i), PAD * g : PAD * g + PAD] * tv[at(g, i), c]
                            for g in range(FRAME)
                        ]
                        while len(terms) > 1:
                            terms = [a + b for a, b in zip(terms[0::2], terms[1::2])]
                        mixed[at(f, i), c] = terms[0]

            for c0, c1 in ((0, 256), (256, 512), (512, D)):
                moved[:, :, c0:c1] = (
                    dot(mixed[0:size, :], wtp[3][:, c0:c1]).astype(BF16).reshape(FRAME, count, c1 - c0)
                )

            @pl.loop(1, FRAME)
            def _(d):
                back_copy(half, d).start()

            ret[pl.ds(pl.multiple_of(start + lax.min(me_f, OWNERS - 1) * count, 16), count), :] = moved[
                me_f
            ]

    load_win.wait()
    load_wout.wait()
    stores = []
    for half, (start, count, inside) in enumerate(HALVES):
        size = count * OWNERS
        rows = pl.ds(start, size)

        @pl.loop(1, FRAME)
        def _(d):
            @pl.when(comes_from_owner(d))
            def _():
                back_copy(half, d).wait_recv()

        @pl.loop(0, OWNERS)
        def _(i):
            part = pl.ds(pl.multiple_of(start + i * count, 16), count)
            second = (first[part, :].astype(F32) + ret[part, :].astype(F32)).astype(BF16)
            x[part, :] = second
            first[part, :] = (norm(second.astype(F32)) * gains[2:3, :]).astype(BF16)

        @pl.loop(0, 2)
        def _(i):
            for j in range(FFH // 512):
                c = pl.ds(pl.multiple_of(i * (FFH // 2) + 256 * j, 256), 256)
                g = pl.ds(pl.multiple_of(FFH + i * (FFH // 2) + 256 * j, 256), 256)
                value = dot(first[rows, :], win[:, c])
                gate = dot(first[rows, :], win[:, g])
                gelu = 0.5 * gate * (1.0 + lax.erf(gate * (1.0 / math.sqrt(2.0))))
                inner[0:size, c] = (value * gelu).astype(BF16)

        for c0, c1 in ((0, 256), (256, 512), (512, D)):
            result[rows, c0:c1] = x[rows, c0:c1].astype(F32) + dot(
                inner[0:size, :], wout[:, c0:c1]
            )
        for j in range(OWNERS):
            store = pltpu.make_async_copy(
                result.at[pl.ds(start + count * j, count)],
                out.at[pl.ds(BLOCK * j + inside, count)],
                sem_out.at[half * OWNERS + j],
            )
            store.start()
            stores.append(store)

    for slot in range(8):
        ref_copy(slot).wait_send()

    for half in range(2):

        @pl.loop(1, FRAME)
        def _(d):
            @pl.when(is_owner(d))
            def _():
                go_copy(half, d).wait_send()

            @pl.when(me_f < OWNERS)
            def _():
                back_copy(half, d).wait_send()

    for store in stores:
        store.wait()


def time_embedding(steps):
    half = D // 2
    freqs = jnp.exp(-math.log(10000.0) * jnp.arange(half, dtype=F32) / half)
    angles = steps.astype(F32)[:, None] * freqs[None, :]
    return jnp.concatenate([jnp.cos(angles), jnp.sin(angles)], axis=-1).astype(BF16)


def per_device(
    latents, timestep, ref_features, norm_gains, w_spatial, w_temporal, w_time, w_in, w_out
):
    emb = time_embedding(timestep)
    vmem = pl.BlockSpec(memory_space=pltpu.VMEM)
    hbm = pl.BlockSpec(memory_space=pl.ANY)
    sems = pltpu.SemaphoreType.DMA
    result = pl.pallas_call(
        body,
        out_shape=jax.ShapeDtypeStruct((ROWS, D), F32),
        in_specs=[hbm, vmem, vmem, vmem, hbm, hbm, hbm, hbm, hbm],
        out_specs=hbm,
        scratch_shapes=[
            pltpu.VMEM((ROWS, D), BF16),
            pltpu.VMEM((ROWS, D), BF16),
            pltpu.VMEM((ROWS, D), BF16),
            pltpu.VMEM((ROWS, WIDE), BF16),
            pltpu.VMEM((WIDE, KEYS_SELF), BF16),
            pltpu.VMEM((KEYS_SELF, WIDE), BF16),
            pltpu.VMEM((REF_PAD, D), BF16),
            pltpu.VMEM((KEYS_REF, D), BF16),
            pltpu.VMEM((WIDE, KEYS_REF), BF16),
            pltpu.VMEM((KEYS_REF, WIDE), BF16),
            pltpu.VMEM((ROWS, WIDE), F32),
            pltpu.VMEM((2, ROWS, KEYS_REF), F32),
            pltpu.VMEM((512, WIDE), BF16),
            pltpu.VMEM((D, WIDE), BF16),
            pltpu.VMEM((D, WIDE), BF16),
            pltpu.VMEM((D, WIDE), BF16),
            pltpu.VMEM((WIDE, D), BF16),
            pltpu.VMEM((4, D, D), BF16),
            pltpu.VMEM((4, D, D), BF16),
            pltpu.VMEM((D, 2 * D), BF16),
            pltpu.VMEM((D, 2 * FFH), BF16),
            pltpu.VMEM((FFH, D), BF16),
            pltpu.VMEM((16, 2 * D), F32),
            pltpu.VMEM((PAD, FRAME * PAD), BF16),
            pltpu.VMEM((FRAME * PAD, PAD), BF16),
            pltpu.VMEM((FRAME, 64, D), BF16),
            pltpu.VMEM((FRAME, 48, D), BF16),
            pltpu.VMEM((FRAME, 64, D), BF16),
            pltpu.VMEM((FRAME, 48, D), BF16),
            pltpu.VMEM((ROWS, D), BF16),
            pltpu.VMEM((448, FFH), BF16),
            sems((2 * OWNERS,)),
            sems((8,)),
            sems((2 * OWNERS,)),
            sems((CLIP,)),
            sems((CLIP,)),
            sems((2 * FRAME,)),
            sems((2 * FRAME,)),
            sems((2 * FRAME,)),
            sems((2 * FRAME,)),
        ],
        compiler_params=pltpu.CompilerParams(
            collective_id=0, has_side_effects=True, vmem_limit_bytes=60 * 1024 * 1024
        ),
        name="block",
    )(latents[0], ref_features, emb, norm_gains, w_spatial, w_temporal, w_time, w_in, w_out)
    return result.astype(BF16)[None]


def solution(mesh):
    placed = (
        P(("clip", "frame"), None, None),
        P(("clip", "frame")),
        P("clip", None),
        P(),
        P(),
        P(),
        P(),
        P(),
        P(),
    )
    return jax.shard_map(
        per_device,
        mesh=mesh,
        in_specs=placed,
        out_specs=P(("clip", "frame"), None, None),
        check_vma=False,
    )
```

```python
import math

import jax
import jax.numpy as jnp
from jax import lax
from jax.experimental import pallas as pl
from jax.experimental.pallas import tpu as pltpu
from jax.sharding import PartitionSpec as P

HEADS = 8
HEAD = 80
D = 640
FFH = 2560
ROWS = 784
PAD = 128
WIDE = HEADS * PAD
CLIP = 16
FRAME = 8
OWNERS = 7
BLOCK = 112
REF = 49
REF_PAD = 64
KEYS_SELF = 768
KEYS_REF = CLIP * REF_PAD
HALVES = ((0, 64, 0), (448, 48, 64))
LOG2E = 1.4426950408889634
FACTOR = LOG2E / math.sqrt(HEAD)
F32 = jnp.float32
BF16 = jnp.bfloat16
MESH = pl.DeviceIdType.MESH


def dot(a, b):
    return jnp.dot(a, b, preferred_element_type=F32)


def norm(wide):
    mean = jnp.mean(wide, axis=-1, keepdims=True)
    centered = wide - mean
    variance = jnp.mean(centered * centered, axis=-1, keepdims=True)
    return centered * lax.rsqrt(variance + 1e-05)


def iota(shape, axis):
    return lax.broadcasted_iota(jnp.int32, shape, axis)


def head_of(column):
    return (column * 52429) >> 22


def attend(rows, size, keys, q, k_t, v, held, floor, finish, per):
    def columns(n):
        return pl.ds(pl.multiple_of(n * PAD, PAD), PAD)

    def scores(n, slot):
        c = columns(n)
        s = dot(q[rows, c], k_t[c, :])
        held[slot, 0:size, 0:keys] = s
        top = jnp.max(s, axis=1, keepdims=True)
        return top if floor is None else jnp.maximum(top, floor(c))

    @pl.loop(0, HEADS // per)
    def _(i):
        top = scores(i * per, 0)
        for n in range(per):
            c = columns(i * per + n)
            later = scores(i * per + n + 1, (n + 1) % 2) if n + 1 < per else None
            weights = jnp.exp2(held[n % 2, 0:size, 0:keys] - top).astype(BF16)
            finish(c, top, dot(weights, v[:, c]))
            top = later


def body(
    lat, ref, emb, gains, w_spatial, w_temporal, w_time, w_in, w_out, out,
    x, first, h, q, k_t, v, ref_stage, ref_all, kr_t, vr, acc, held, attn, wq, wk, wv, wo,
    ws, wt, wtime, win, wout, mod, spread, gather,
    recv_a, recv_b, moved_a, moved_b, ret, inner,
    sem_x, sem_w, sem_out, ref_send, ref_recv, go_send, go_recv, back_send, back_recv,
):
    swap = ws.at[0]
    wtp = (ws.at[1], ws.at[2], ws.at[3], wt.at[0])
    tq, tk, tv, mixed = (w.at[0:512, 0:D] for w in (wq, wk, wv, wtime))
    result = ret

    me_c = lax.axis_index("clip")
    me_f = lax.axis_index("frame")

    loads_x = []
    for half, (start, count, inside) in enumerate(HALVES):
        for j in range(OWNERS):
            loads_x.append(
                pltpu.make_async_copy(
                    lat.at[pl.ds(BLOCK * j + inside, count)],
                    x.at[pl.ds(start + count * j, count)],
                    sem_x.at[half * OWNERS + j],
                )
            )
    loads_ws = [pltpu.make_async_copy(w_spatial.at[i], ws.at[i], sem_w.at[4 + i]) for i in range(4)]
    load_wtime = pltpu.make_async_copy(w_time, wtime, sem_w.at[0])
    load_wt = pltpu.make_async_copy(w_temporal, wt, sem_w.at[1])
    load_win = pltpu.make_async_copy(w_in, win, sem_w.at[2])
    load_wout = pltpu.make_async_copy(w_out, wout, sem_w.at[3])
    for load in loads_x:
        load.start()
    for load in loads_ws:
        load.start()

    ref_stage[...] = jnp.zeros_like(ref_stage)
    ref_stage[0:REF, :] = ref[...]

    z_hi, y, core = lax.div(me_c, 8), lax.rem(lax.div(me_c, 2), 4), lax.rem(me_c, 2)
    other_frame = me_f + 1 - 2 * lax.rem(me_f, 2)
    sibling = me_c + 1 - 2 * core
    routes = [(0, dy) for dy in (1, 2, 3)] + [(1, dy) for dy in range(4)]

    def clip_of(far, dy, at_core):
        half = (1 - z_hi) if far else z_hi
        return half * 8 + lax.rem(y + dy, 4) * 2 + at_core

    targets = [(clip_of(far, dy, core), other_frame if far else me_f) for far, dy in routes]
    targets.append((sibling, me_f))
    barrier = pltpu.get_barrier_semaphore()
    for clip, frame in targets:
        pl.semaphore_signal(
            barrier, inc=1, device_id={"clip": clip, "frame": frame}, device_id_type=MESH
        )

    @pl.loop(1, FRAME)
    def _(d):
        pl.semaphore_signal(
            barrier,
            inc=1,
            device_id={"clip": me_c, "frame": lax.rem(me_f + d, FRAME)},
            device_id_type=MESH,
        )

    pl.semaphore_wait(barrier, len(targets) + FRAME - 1)

    def ref_rows(clip):
        return ref_all.at[pl.ds(pl.multiple_of(clip * REF_PAD, REF_PAD), REF_PAD)]

    def ref_copy(slot):
        clip, frame = targets[slot]
        return pltpu.make_async_remote_copy(
            src_ref=ref_stage,
            dst_ref=ref_rows(me_c),
            send_sem=ref_send.at[slot],
            recv_sem=ref_recv.at[slot],
            device_id={"clip": clip, "frame": frame},
            device_id_type=MESH,
        )

    def ref_forward(slot):
        far, dy = routes[slot]
        piece = ref_rows(clip_of(far, 4 - dy, core))
        return pltpu.make_async_remote_copy(
            src_ref=piece,
            dst_ref=piece,
            send_sem=ref_send.at[8 + slot],
            recv_sem=ref_recv.at[8 + slot],
            device_id={"clip": sibling, "frame": me_f},
            device_id_type=MESH,
        )

    for slot in range(8):
        ref_copy(slot).start()

    ref_all[pl.ds(pl.multiple_of(me_c * REF_PAD, REF_PAD), REF_PAD), :] = ref_stage[...]

    wq[...] = jnp.zeros_like(wq)
    wk[...] = jnp.zeros_like(wk)
    wv[...] = jnp.zeros_like(wv)
    wo[...] = jnp.zeros_like(wo)

    for load in loads_x:
        load.wait()

    @pl.loop(0, ROWS // BLOCK)
    def _(i):
        rows = pl.ds(pl.multiple_of(i * BLOCK, BLOCK), BLOCK)
        h[rows, :] = (norm(x[rows, :].astype(F32)) * gains[0:1, :]).astype(BF16)

    for i, target in enumerate((wq, wk, wv)):
        loads_ws[i].wait()
        for n in range(HEADS):
            target[:, PAD * n : PAD * n + HEAD] = ws[i, :, HEAD * n : HEAD * n + HEAD]
    loads_ws[3].wait()
    for n in range(HEADS):
        wo[PAD * n : PAD * n + HEAD, :] = ws[3, HEAD * n : HEAD * n + HEAD, :]
    load_wtime.start()
    load_wt.start()
    load_win.start()
    load_wout.start()

    for j in range(WIDE // 256):
        c = pl.ds(j * 256, 256)
        lane = iota((1, 256), 1) & (PAD - 1)
        q[:, c] = jnp.where(lane == HEAD, 1.0, dot(h[...], wq[:, c]) * FACTOR).astype(BF16)
        k_t[c, :] = dot(h[0:KEYS_SELF, :], wk[:, c]).astype(BF16).T
        v[:, c] = jnp.where(lane == HEAD, 1.0, dot(h[0:KEYS_SELF, :], wv[:, c])).astype(BF16)

    def attend_own(half):
        start, count, _ = HALVES[half]
        rows = pl.ds(start, count * OWNERS)

        def own(c, top, o):
            acc[rows, c] = jnp.where(iota((1, PAD), 1) == HEAD + 1, top, o)

        attend(rows, count * OWNERS, KEYS_SELF, q, k_t, v, held, None, own, 4)

    for slot in range(7):
        ref_copy(slot).wait_recv()
        ref_forward(slot).start()
    attend_own(0)

    load_wtime.wait()
    mod[...] = dot(jnp.broadcast_to(emb[...], (16, D)), wtime[...])

    ref_copy(7).wait_recv()
    for slot in range(7):
        ref_forward(slot).wait()

    row = iota((PAD, 16), 0)
    tail = iota((PAD, 16), 1)
    place = ((row < REF_PAD) & (row == tail + REF)) | ((row == REF_PAD + REF) & (tail == 15))
    placed = dot(place.astype(F32).astype(BF16), h[KEYS_SELF:ROWS, :])
    ref_all[0:PAD, :] = (ref_all[0:PAD, :].astype(F32) + placed).astype(BF16)

    for j in range(WIDE // 256):
        c = pl.ds(j * 256, 256)
        lane = iota((1, 256), 1) & (PAD - 1)
        key = iota((KEYS_REF, 1), 0)
        valid = ((key & (REF_PAD - 1)) < REF) | (key < REF_PAD) | (key == REF_PAD + REF)
        mask = jnp.where(valid, 0.0, -1e30)
        kr_t[c, :] = jnp.where(lane == HEAD, mask, dot(ref_all[...], wk[:, c])).astype(BF16).T
        vr[:, c] = jnp.where(lane == HEAD, 1.0, dot(ref_all[...], wv[:, c])).astype(BF16)

    def go_copy(half, d):
        start, count, _ = HALVES[half]
        target = lax.rem(me_f + d, FRAME)
        block = lax.min(target, OWNERS - 1)
        return pltpu.make_async_remote_copy(
            src_ref=h.at[pl.ds(pl.multiple_of(start + block * count, 16), count)],
            dst_ref=(recv_a, recv_b)[half].at[me_f],
            send_sem=go_send.at[half * FRAME + d],
            recv_sem=go_recv.at[half * FRAME + d],
            device_id={"clip": me_c, "frame": target},
            device_id_type=MESH,
        )

    def is_owner(d):
        return lax.rem(me_f + d, FRAME) < OWNERS

    def comes_from_owner(d):
        return lax.rem(me_f + FRAME - d, FRAME) < OWNERS

    for half, (start, count, _) in enumerate(HALVES):
        size = count * OWNERS
        rows = pl.ds(start, size)

        if half == 1:
            attend_own(1)

        def own_top(c):
            return acc[rows, c][:, HEAD + 1 : HEAD + 2]

        def merge(c, top, o):
            before = acc[rows, c]
            o = o + before * jnp.exp2(before[:, HEAD + 1 : HEAD + 2] - top)
            attn[0:size, c] = (o * (1.0 / o[:, HEAD : HEAD + 1])).astype(BF16)

        attend(rows, size, KEYS_REF, q, kr_t, vr, held, own_top, merge, 8)

        for c0, c1 in ((0, 256), (256, 512), (512, D)):
            first[rows, c0:c1] = (
                x[rows, c0:c1].astype(F32) + dot(attn[0:size, :], wo[:, c0:c1])
            ).astype(BF16)

        @pl.loop(0, OWNERS)
        def _(i):
            part = pl.ds(pl.multiple_of(start + i * count, 16), count)
            normed = norm(first[part, :].astype(F32)) * gains[1:2, :]
            h[part, :] = (normed * (1.0 + mod[0:1, D:]) + mod[0:1, :D]).astype(BF16)

        @pl.loop(1, FRAME)
        def _(d):
            @pl.when(is_owner(d))
            def _():
                go_copy(half, d).start()

        @pl.when(me_f < OWNERS)
        def _():
            (recv_a, recv_b)[half][me_f] = h[
                pl.ds(pl.multiple_of(start + lax.min(me_f, OWNERS - 1) * count, 16), count), :
            ]

    def back_copy(half, d):
        start, count, _ = HALVES[half]
        target = lax.rem(me_f + d, FRAME)
        return pltpu.make_async_remote_copy(
            src_ref=(moved_a, moved_b)[half].at[target],
            dst_ref=ret.at[pl.ds(pl.multiple_of(start + lax.min(me_f, OWNERS - 1) * count, 16), count)],
            send_sem=back_send.at[half * FRAME + d],
            recv_sem=back_recv.at[half * FRAME + d],
            device_id={"clip": me_c, "frame": target},
            device_id_type=MESH,
        )

    load_wt.wait()
    column = iota((D, D), 1)
    source = HEAD * ((column & (PAD - 1)) >> 4) + 16 * (column >> 7) + (column & 15)
    swap[...] = (iota((D, D), 0) == source).astype(F32).astype(BF16)
    for i in range(3):
        for c0, c1 in ((0, 256), (256, 512), (512, D)):
            wtp[i][:, c0:c1] = dot(wt[i], swap[:, c0:c1]).astype(BF16)
    for n in range(HEADS):
        for r in range(D // PAD):
            wtp[3][PAD * r + 16 * n : PAD * r + 16 * n + 16, :] = wt[
                3, HEAD * n + 16 * r : HEAD * n + 16 * r + 16, :
            ]
    place = iota((FRAME * PAD, PAD), 0)
    pair = FRAME * (place >> 7) + ((place & (PAD - 1)) >> 4)
    gather[...] = ((iota((FRAME * PAD, PAD), 1) & 63) == pair).astype(F32).astype(BF16)
    place = iota((PAD, FRAME * PAD), 1)
    pair = FRAME * (place >> 7) + ((place & (PAD - 1)) >> 4)
    spread[...] = (iota((PAD, FRAME * PAD), 0) == pair).astype(F32).astype(BF16)

    @pl.when(me_f < OWNERS)
    def _():
        for half, (start, count, _) in enumerate(HALVES):
            size = count * FRAME
            recv = (recv_a, recv_b)[half]
            moved = (moved_a, moved_b)[half]

            @pl.loop(1, FRAME)
            def _(d):
                go_copy(half, d).wait_recv()

            for c0, c1 in ((0, 256), (256, 512), (512, D)):
                states = recv[...].reshape(size, D)
                tq[0:size, c0:c1] = (dot(states, wtp[0][:, c0:c1]) * FACTOR).astype(BF16)
                tk[0:size, c0:c1] = dot(states, wtp[1][:, c0:c1]).astype(BF16)
                tv[0:size, c0:c1] = dot(states, wtp[2][:, c0:c1]).astype(BF16)

            def at(f, i):
                return pl.ds(pl.multiple_of(f * count + 16 * i, 16), 16)

            @pl.loop(0, count // 16)
            def _(i):
                for f in range(FRAME):
                    queries = tq[at(f, i), :]
                    for g in range(FRAME):
                        pairs = queries * tk[at(g, i), :]
                        part = pairs[:, 0:PAD]
                        for r in range(1, D // PAD):
                            part = part + pairs[:, PAD * r : PAD * r + PAD]
                        attn[at(f, i), PAD * g : PAD * g + PAD] = part

            s = dot(attn[0:size, :], gather[...])
            top = s
            for shift in (8, 16, 32):
                top = jnp.maximum(top, pltpu.roll(top, shift, 1))
            e = jnp.exp2(s - top)
            total = e
            for shift in (8, 16, 32):
                total = total + pltpu.roll(total, shift, 1)
            weights = (e / total).astype(BF16)
            for c0 in range(0, FRAME * PAD, 256):
                attn[0:size, c0 : c0 + 256] = dot(weights, spread[:, c0 : c0 + 256]).astype(BF16)

            @pl.loop(0, count // 16)
            def _(i):
                for f in range(FRAME):
                    for r in range(D // PAD):
                        c = slice(PAD * r, PAD * r + PAD)
                        terms = [
                            attn[at(f, i), PAD * g : PAD * g + PAD] * tv[at(g, i), c]
                            for g in range(FRAME)
                        ]
                        while len(terms) > 1:
                            terms = [a + b for a, b in zip(terms[0::2], terms[1::2])]
                        mixed[at(f, i), c] = terms[0]

            for c0, c1 in ((0, 256), (256, 512), (512, D)):
                moved[:, :, c0:c1] = (
                    dot(mixed[0:size, :], wtp[3][:, c0:c1]).astype(BF16).reshape(FRAME, count, c1 - c0)
                )

            @pl.loop(1, FRAME)
            def _(d):
                back_copy(half, d).start()

            ret[pl.ds(pl.multiple_of(start + lax.min(me_f, OWNERS - 1) * count, 16), count), :] = moved[
                me_f
            ]

    load_win.wait()
    load_wout.wait()
    stores = []
    for half, (start, count, inside) in enumerate(HALVES):
        size = count * OWNERS
        rows = pl.ds(start, size)

        @pl.loop(1, FRAME)
        def _(d):
            @pl.when(comes_from_owner(d))
            def _():
                back_copy(half, d).wait_recv()

        @pl.loop(0, OWNERS)
        def _(i):
            part = pl.ds(pl.multiple_of(start + i * count, 16), count)
            second = (first[part, :].astype(F32) + ret[part, :].astype(F32)).astype(BF16)
            x[part, :] = second
            first[part, :] = (norm(second.astype(F32)) * gains[2:3, :]).astype(BF16)

        @pl.loop(0, 2)
        def _(i):
            for j in range(FFH // 512):
                c = pl.ds(pl.multiple_of(i * (FFH // 2) + 256 * j, 256), 256)
                g = pl.ds(pl.multiple_of(FFH + i * (FFH // 2) + 256 * j, 256), 256)
                value = dot(first[rows, :], win[:, c])
                gate = dot(first[rows, :], win[:, g])
                gelu = 0.5 * gate * (1.0 + lax.erf(gate * (1.0 / math.sqrt(2.0))))
                inner[0:size, c] = (value * gelu).astype(BF16)

        for c0, c1 in ((0, 256), (256, 512), (512, D)):
            result[rows, c0:c1] = (
                x[rows, c0:c1].astype(F32) + dot(inner[0:size, :], wout[:, c0:c1])
            ).astype(BF16)
        for j in range(OWNERS):
            store = pltpu.make_async_copy(
                result.at[pl.ds(start + count * j, count)],
                out.at[pl.ds(BLOCK * j + inside, count)],
                sem_out.at[half * OWNERS + j],
            )
            store.start()
            stores.append(store)

    for slot in range(8):
        ref_copy(slot).wait_send()

    for half in range(2):

        @pl.loop(1, FRAME)
        def _(d):
            @pl.when(is_owner(d))
            def _():
                go_copy(half, d).wait_send()

            @pl.when(me_f < OWNERS)
            def _():
                back_copy(half, d).wait_send()

    for store in stores:
        store.wait()


def time_embedding(steps):
    half = D // 2
    freqs = jnp.exp(-math.log(10000.0) * jnp.arange(half, dtype=F32) / half)
    angles = steps.astype(F32)[:, None] * freqs[None, :]
    return jnp.concatenate([jnp.cos(angles), jnp.sin(angles)], axis=-1).astype(BF16)


def per_device(
    latents, timestep, ref_features, norm_gains, w_spatial, w_temporal, w_time, w_in, w_out
):
    emb = time_embedding(timestep)
    vmem = pl.BlockSpec(memory_space=pltpu.VMEM)
    hbm = pl.BlockSpec(memory_space=pl.ANY)
    sems = pltpu.SemaphoreType.DMA
    result = pl.pallas_call(
        body,
        out_shape=jax.ShapeDtypeStruct((ROWS, D), BF16),
        in_specs=[hbm, vmem, vmem, vmem, hbm, hbm, hbm, hbm, hbm],
        out_specs=hbm,
        scratch_shapes=[
            pltpu.VMEM((ROWS, D), BF16),
            pltpu.VMEM((ROWS, D), BF16),
            pltpu.VMEM((ROWS, D), BF16),
            pltpu.VMEM((ROWS, WIDE), BF16),
            pltpu.VMEM((WIDE, KEYS_SELF), BF16),
            pltpu.VMEM((KEYS_SELF, WIDE), BF16),
            pltpu.VMEM((REF_PAD, D), BF16),
            pltpu.VMEM((KEYS_REF, D), BF16),
            pltpu.VMEM((WIDE, KEYS_REF), BF16),
            pltpu.VMEM((KEYS_REF, WIDE), BF16),
            pltpu.VMEM((ROWS, WIDE), F32),
            pltpu.VMEM((2, ROWS, KEYS_REF), F32),
            pltpu.VMEM((512, WIDE), BF16),
            pltpu.VMEM((D, WIDE), BF16),
            pltpu.VMEM((D, WIDE), BF16),
            pltpu.VMEM((D, WIDE), BF16),
            pltpu.VMEM((WIDE, D), BF16),
            pltpu.VMEM((4, D, D), BF16),
            pltpu.VMEM((4, D, D), BF16),
            pltpu.VMEM((D, 2 * D), BF16),
            pltpu.VMEM((D, 2 * FFH), BF16),
            pltpu.VMEM((FFH, D), BF16),
            pltpu.VMEM((16, 2 * D), F32),
            pltpu.VMEM((PAD, FRAME * PAD), BF16),
            pltpu.VMEM((FRAME * PAD, PAD), BF16),
            pltpu.VMEM((FRAME, 64, D), BF16),
            pltpu.VMEM((FRAME, 48, D), BF16),
            pltpu.VMEM((FRAME, 64, D), BF16),
            pltpu.VMEM((FRAME, 48, D), BF16),
            pltpu.VMEM((ROWS, D), BF16),
            pltpu.VMEM((448, FFH), BF16),
            sems((2 * OWNERS,)),
            sems((8,)),
            sems((2 * OWNERS,)),
            sems((CLIP,)),
            sems((CLIP,)),
            sems((2 * FRAME,)),
            sems((2 * FRAME,)),
            sems((2 * FRAME,)),
            sems((2 * FRAME,)),
        ],
        compiler_params=pltpu.CompilerParams(
            collective_id=0, has_side_effects=True, vmem_limit_bytes=60 * 1024 * 1024
        ),
        name="block",
    )(latents[0], ref_features, emb, norm_gains, w_spatial, w_temporal, w_time, w_in, w_out)
    return result[None]


def solution(mesh):
    placed = (
        P(("clip", "frame"), None, None),
        P(("clip", "frame")),
        P("clip", None),
        P(),
        P(),
        P(),
        P(),
        P(),
        P(),
    )
    return jax.shard_map(
        per_device,
        mesh=mesh,
        in_specs=placed,
        out_specs=P(("clip", "frame"), None, None),
        check_vma=False,
    )
```

```python
import math

import jax
import jax.numpy as jnp
from jax import lax
from jax.experimental import pallas as pl
from jax.experimental.pallas import tpu as pltpu
from jax.sharding import PartitionSpec as P

HEADS = 8
HEAD = 80
D = 640
FFH = 2560
ROWS = 784
PAD = 128
WIDE = HEADS * PAD
CLIP = 16
FRAME = 8
OWNERS = 7
BLOCK = 112
REF = 49
REF_PAD = 64
KEYS_SELF = 768
KEYS_REF = CLIP * REF_PAD
HALVES = ((0, 64, 0), (448, 48, 64))
LOG2E = 1.4426950408889634
FACTOR = LOG2E / math.sqrt(HEAD)
F32 = jnp.float32
BF16 = jnp.bfloat16
MESH = pl.DeviceIdType.MESH


def dot(a, b):
    return jnp.dot(a, b, preferred_element_type=F32)


def norm(wide):
    mean = jnp.mean(wide, axis=-1, keepdims=True)
    centered = wide - mean
    variance = jnp.mean(centered * centered, axis=-1, keepdims=True)
    return centered * lax.rsqrt(variance + 1e-05)


def iota(shape, axis):
    return lax.broadcasted_iota(jnp.int32, shape, axis)


def head_of(column):
    return (column * 52429) >> 22


def attend(rows, size, keys, q, k_t, v, held, floor, finish, per):
    def columns(n):
        return pl.ds(pl.multiple_of(n * PAD, PAD), PAD)

    def scores(n, slot):
        c = columns(n)
        s = dot(q[rows, c], k_t[c, :])
        held[slot, 0:size, 0:keys] = s
        top = jnp.max(s, axis=1, keepdims=True)
        return top if floor is None else jnp.maximum(top, floor(c))

    @pl.loop(0, HEADS // per)
    def _(i):
        top = scores(i * per, 0)
        for n in range(per):
            c = columns(i * per + n)
            later = scores(i * per + n + 1, (n + 1) % 2) if n + 1 < per else None
            weights = jnp.exp2(held[n % 2, 0:size, 0:keys] - top).astype(BF16)
            finish(c, top, dot(weights, v[:, c]))
            top = later


def body(
    lat, ref, emb, gains, w_spatial, w_temporal, w_time, w_in, w_out, out,
    x, first, h, q, k_t, v, ref_stage, ref_all, kr_t, vr, acc, held, attn, wq, wk, wv, wo,
    ws, wt, wtime, win, wout, mod, spread, gather,
    recv_a, recv_b, moved_a, moved_b, ret, inner,
    sem_x, sem_w, sem_out, ref_send, ref_recv, go_send, go_recv, back_send, back_recv,
):
    swap = ws.at[0]
    wtp = (ws.at[1], ws.at[2], ws.at[3], wt.at[0])
    tq, tk, tv, mixed = (w.at[0:512, 0:D] for w in (wq, wk, wv, wtime))
    result = ret

    me_c = lax.axis_index("clip")
    me_f = lax.axis_index("frame")

    loads_x = []
    for half, (start, count, inside) in enumerate(HALVES):
        for j in range(OWNERS):
            loads_x.append(
                pltpu.make_async_copy(
                    lat.at[pl.ds(BLOCK * j + inside, count)],
                    x.at[pl.ds(start + count * j, count)],
                    sem_x.at[half * OWNERS + j],
                )
            )
    loads_ws = [pltpu.make_async_copy(w_spatial.at[i], ws.at[i], sem_w.at[4 + i]) for i in range(4)]
    load_wtime = pltpu.make_async_copy(w_time, wtime, sem_w.at[0])
    load_wt = pltpu.make_async_copy(w_temporal, wt, sem_w.at[1])
    load_win = pltpu.make_async_copy(w_in, win, sem_w.at[2])
    load_wout = pltpu.make_async_copy(w_out, wout, sem_w.at[3])
    for load in loads_x:
        load.start()
    for load in loads_ws:
        load.start()

    ref_stage[...] = jnp.zeros_like(ref_stage)
    ref_stage[0:REF, :] = ref[...]

    z_hi, y, core = lax.div(me_c, 8), lax.rem(lax.div(me_c, 2), 4), lax.rem(me_c, 2)
    other_frame = me_f + 1 - 2 * lax.rem(me_f, 2)
    sibling = me_c + 1 - 2 * core
    routes = [(0, dy) for dy in (1, 2, 3)] + [(1, dy) for dy in range(4)]

    def clip_of(far, dy, at_core):
        half = (1 - z_hi) if far else z_hi
        return half * 8 + lax.rem(y + dy, 4) * 2 + at_core

    targets = [(clip_of(far, dy, core), other_frame if far else me_f) for far, dy in routes]
    targets.append((sibling, me_f))
    barrier = pltpu.get_barrier_semaphore()
    for clip, frame in targets:
        pl.semaphore_signal(
            barrier, inc=1, device_id={"clip": clip, "frame": frame}, device_id_type=MESH
        )

    @pl.loop(1, FRAME)
    def _(d):
        pl.semaphore_signal(
            barrier,
            inc=1,
            device_id={"clip": me_c, "frame": lax.rem(me_f + d, FRAME)},
            device_id_type=MESH,
        )

    pl.semaphore_wait(barrier, len(targets) + FRAME - 1)

    def ref_rows(clip):
        return ref_all.at[pl.ds(pl.multiple_of(clip * REF_PAD, REF_PAD), REF_PAD)]

    def ref_copy(slot):
        clip, frame = targets[slot]
        return pltpu.make_async_remote_copy(
            src_ref=ref_stage,
            dst_ref=ref_rows(me_c),
            send_sem=ref_send.at[slot],
            recv_sem=ref_recv.at[slot],
            device_id={"clip": clip, "frame": frame},
            device_id_type=MESH,
        )

    def ref_forward(slot):
        far, dy = routes[slot]
        piece = ref_rows(clip_of(far, 4 - dy, core))
        return pltpu.make_async_remote_copy(
            src_ref=piece,
            dst_ref=piece,
            send_sem=ref_send.at[8 + slot],
            recv_sem=ref_recv.at[8 + slot],
            device_id={"clip": sibling, "frame": me_f},
            device_id_type=MESH,
        )

    for slot in range(8):
        ref_copy(slot).start()

    ref_all[pl.ds(pl.multiple_of(me_c * REF_PAD, REF_PAD), REF_PAD), :] = ref_stage[...]

    wq[...] = jnp.zeros_like(wq)
    wk[...] = jnp.zeros_like(wk)
    wv[...] = jnp.zeros_like(wv)
    wo[...] = jnp.zeros_like(wo)

    for load in loads_x:
        load.wait()

    @pl.loop(0, ROWS // BLOCK)
    def _(i):
        rows = pl.ds(pl.multiple_of(i * BLOCK, BLOCK), BLOCK)
        h[rows, :] = (norm(x[rows, :].astype(F32)) * gains[0:1, :]).astype(BF16)

    for i, target in enumerate((wq, wk, wv)):
        loads_ws[i].wait()
        for n in range(HEADS):
            target[:, PAD * n : PAD * n + HEAD] = ws[i, :, HEAD * n : HEAD * n + HEAD]
    loads_ws[3].wait()
    for n in range(HEADS):
        wo[PAD * n : PAD * n + HEAD, :] = ws[3, HEAD * n : HEAD * n + HEAD, :]
    load_wtime.start()
    load_wt.start()
    load_win.start()
    load_wout.start()

    for j in range(WIDE // 256):
        c = pl.ds(j * 256, 256)
        lane = iota((1, 256), 1) & (PAD - 1)
        q[:, c] = jnp.where(lane == HEAD, 1.0, dot(h[...], wq[:, c]) * FACTOR).astype(BF16)
        k_t[c, :] = dot(h[0:KEYS_SELF, :], wk[:, c]).astype(BF16).T
        v[:, c] = jnp.where(lane == HEAD, 1.0, dot(h[0:KEYS_SELF, :], wv[:, c])).astype(BF16)

    def attend_own(half):
        start, count, _ = HALVES[half]
        rows = pl.ds(start, count * OWNERS)

        def own(c, top, o):
            acc[rows, c] = jnp.where(iota((1, PAD), 1) == HEAD + 1, top, o)

        attend(rows, count * OWNERS, KEYS_SELF, q, k_t, v, held, None, own, 4)

    for slot in range(7):
        ref_copy(slot).wait_recv()
        ref_forward(slot).start()
    attend_own(0)

    load_wtime.wait()
    mod[...] = dot(jnp.broadcast_to(emb[...], (16, D)), wtime[...])

    ref_copy(7).wait_recv()
    for slot in range(7):
        ref_forward(slot).wait()

    row = iota((PAD, 16), 0)
    tail = iota((PAD, 16), 1)
    place = ((row < REF_PAD) & (row == tail + REF)) | ((row == REF_PAD + REF) & (tail == 15))
    placed = dot(place.astype(F32).astype(BF16), h[KEYS_SELF:ROWS, :])
    ref_all[0:PAD, :] = (ref_all[0:PAD, :].astype(F32) + placed).astype(BF16)

    for j in range(WIDE // 256):
        c = pl.ds(j * 256, 256)
        lane = iota((1, 256), 1) & (PAD - 1)
        key = iota((KEYS_REF, 1), 0)
        valid = ((key & (REF_PAD - 1)) < REF) | (key < REF_PAD) | (key == REF_PAD + REF)
        mask = jnp.where(valid, 0.0, -1e30)
        kr_t[c, :] = jnp.where(lane == HEAD, mask, dot(ref_all[...], wk[:, c])).astype(BF16).T
        vr[:, c] = jnp.where(lane == HEAD, 1.0, dot(ref_all[...], wv[:, c])).astype(BF16)

    def go_copy(half, d):
        start, count, _ = HALVES[half]
        target = lax.rem(me_f + d, FRAME)
        block = lax.min(target, OWNERS - 1)
        return pltpu.make_async_remote_copy(
            src_ref=h.at[pl.ds(pl.multiple_of(start + block * count, 16), count)],
            dst_ref=(recv_a, recv_b)[half].at[me_f],
            send_sem=go_send.at[half * FRAME + d],
            recv_sem=go_recv.at[half * FRAME + d],
            device_id={"clip": me_c, "frame": target},
            device_id_type=MESH,
        )

    def is_owner(d):
        return lax.rem(me_f + d, FRAME) < OWNERS

    def comes_from_owner(d):
        return lax.rem(me_f + FRAME - d, FRAME) < OWNERS

    for half, (start, count, _) in enumerate(HALVES):
        size = count * OWNERS
        rows = pl.ds(start, size)

        if half == 1:
            attend_own(1)

        def own_top(c):
            return acc[rows, c][:, HEAD + 1 : HEAD + 2]

        def merge(c, top, o):
            before = acc[rows, c]
            o = o + before * jnp.exp2(before[:, HEAD + 1 : HEAD + 2] - top)
            attn[0:size, c] = (o * (1.0 / o[:, HEAD : HEAD + 1])).astype(BF16)

        attend(rows, size, KEYS_REF, q, kr_t, vr, held, own_top, merge, 8)

        for c0, c1 in ((0, 256), (256, 512), (512, D)):
            first[rows, c0:c1] = (
                x[rows, c0:c1].astype(F32) + dot(attn[0:size, :], wo[:, c0:c1])
            ).astype(BF16)

        @pl.loop(1, FRAME + 1)
        def _(d):
            @pl.when(is_owner(d))
            def _():
                block = lax.min(lax.rem(me_f + d, FRAME), OWNERS - 1)
                part = pl.ds(pl.multiple_of(start + block * count, 16), count)
                normed = norm(first[part, :].astype(F32)) * gains[1:2, :]
                h[part, :] = (normed * (1.0 + mod[0:1, D:]) + mod[0:1, :D]).astype(BF16)

                @pl.when(d < FRAME)
                def _():
                    go_copy(half, d).start()

        @pl.when(me_f < OWNERS)
        def _():
            (recv_a, recv_b)[half][me_f] = h[
                pl.ds(pl.multiple_of(start + lax.min(me_f, OWNERS - 1) * count, 16), count), :
            ]

    def back_copy(half, d):
        start, count, _ = HALVES[half]
        target = lax.rem(me_f + d, FRAME)
        return pltpu.make_async_remote_copy(
            src_ref=(moved_a, moved_b)[half].at[target],
            dst_ref=ret.at[pl.ds(pl.multiple_of(start + lax.min(me_f, OWNERS - 1) * count, 16), count)],
            send_sem=back_send.at[half * FRAME + d],
            recv_sem=back_recv.at[half * FRAME + d],
            device_id={"clip": me_c, "frame": target},
            device_id_type=MESH,
        )

    load_wt.wait()
    column = iota((D, D), 1)
    source = HEAD * ((column & (PAD - 1)) >> 4) + 16 * (column >> 7) + (column & 15)
    swap[...] = (iota((D, D), 0) == source).astype(F32).astype(BF16)
    for i in range(3):
        for c0, c1 in ((0, 256), (256, 512), (512, D)):
            wtp[i][:, c0:c1] = dot(wt[i], swap[:, c0:c1]).astype(BF16)
    for n in range(HEADS):
        for r in range(D // PAD):
            wtp[3][PAD * r + 16 * n : PAD * r + 16 * n + 16, :] = wt[
                3, HEAD * n + 16 * r : HEAD * n + 16 * r + 16, :
            ]
    place = iota((FRAME * PAD, PAD), 0)
    pair = FRAME * (place >> 7) + ((place & (PAD - 1)) >> 4)
    gather[...] = ((iota((FRAME * PAD, PAD), 1) & 63) == pair).astype(F32).astype(BF16)
    place = iota((PAD, FRAME * PAD), 1)
    pair = FRAME * (place >> 7) + ((place & (PAD - 1)) >> 4)
    spread[...] = (iota((PAD, FRAME * PAD), 0) == pair).astype(F32).astype(BF16)

    @pl.when(me_f < OWNERS)
    def _():
        for half, (start, count, _) in enumerate(HALVES):
            size = count * FRAME
            recv = (recv_a, recv_b)[half]
            moved = (moved_a, moved_b)[half]

            @pl.loop(1, FRAME)
            def _(d):
                go_copy(half, d).wait_recv()

            for c0, c1 in ((0, 256), (256, 512), (512, D)):
                states = recv[...].reshape(size, D)
                tq[0:size, c0:c1] = (dot(states, wtp[0][:, c0:c1]) * FACTOR).astype(BF16)
                tk[0:size, c0:c1] = dot(states, wtp[1][:, c0:c1]).astype(BF16)
                tv[0:size, c0:c1] = dot(states, wtp[2][:, c0:c1]).astype(BF16)

            def at(f, i):
                return pl.ds(pl.multiple_of(f * count + 16 * i, 16), 16)

            @pl.loop(0, count // 16)
            def _(i):
                for f in range(FRAME):
                    queries = tq[at(f, i), :]
                    for g in range(FRAME):
                        pairs = queries * tk[at(g, i), :]
                        part = pairs[:, 0:PAD]
                        for r in range(1, D // PAD):
                            part = part + pairs[:, PAD * r : PAD * r + PAD]
                        attn[at(f, i), PAD * g : PAD * g + PAD] = part

            s = dot(attn[0:size, :], gather[...])
            top = s
            for shift in (8, 16, 32):
                top = jnp.maximum(top, pltpu.roll(top, shift, 1))
            e = jnp.exp2(s - top)
            total = e
            for shift in (8, 16, 32):
                total = total + pltpu.roll(total, shift, 1)
            weights = (e / total).astype(BF16)
            for c0 in range(0, FRAME * PAD, 256):
                attn[0:size, c0 : c0 + 256] = dot(weights, spread[:, c0 : c0 + 256]).astype(BF16)

            @pl.loop(0, count // 16)
            def _(i):
                for f in range(FRAME):
                    for r in range(D // PAD):
                        c = slice(PAD * r, PAD * r + PAD)
                        terms = [
                            attn[at(f, i), PAD * g : PAD * g + PAD] * tv[at(g, i), c]
                            for g in range(FRAME)
                        ]
                        while len(terms) > 1:
                            terms = [a + b for a, b in zip(terms[0::2], terms[1::2])]
                        mixed[at(f, i), c] = terms[0]

            for c0, c1 in ((0, 256), (256, 512), (512, D)):
                moved[:, :, c0:c1] = (
                    dot(mixed[0:size, :], wtp[3][:, c0:c1]).astype(BF16).reshape(FRAME, count, c1 - c0)
                )

            @pl.loop(1, FRAME)
            def _(d):
                back_copy(half, d).start()

            ret[pl.ds(pl.multiple_of(start + lax.min(me_f, OWNERS - 1) * count, 16), count), :] = moved[
                me_f
            ]

    load_win.wait()
    load_wout.wait()
    stores = []
    for half, (start, count, inside) in enumerate(HALVES):
        size = count * OWNERS
        rows = pl.ds(start, size)

        @pl.loop(0, FRAME)
        def _(d):
            @pl.when(comes_from_owner(d))
            def _():
                @pl.when(d > 0)
                def _():
                    back_copy(half, d).wait_recv()

                block = lax.min(lax.rem(me_f + FRAME - d, FRAME), OWNERS - 1)
                part = pl.ds(pl.multiple_of(start + block * count, 16), count)
                second = (first[part, :].astype(F32) + ret[part, :].astype(F32)).astype(BF16)
                x[part, :] = second
                first[part, :] = (norm(second.astype(F32)) * gains[2:3, :]).astype(BF16)

        @pl.loop(0, 2)
        def _(i):
            for j in range(FFH // 512):
                c = pl.ds(pl.multiple_of(i * (FFH // 2) + 256 * j, 256), 256)
                g = pl.ds(pl.multiple_of(FFH + i * (FFH // 2) + 256 * j, 256), 256)
                value = dot(first[rows, :], win[:, c])
                gate = dot(first[rows, :], win[:, g])
                gelu = 0.5 * gate * (1.0 + lax.erf(gate * (1.0 / math.sqrt(2.0))))
                inner[0:size, c] = (value * gelu).astype(BF16)

        for c0, c1 in ((0, 256), (256, 512), (512, D)):
            result[rows, c0:c1] = (
                x[rows, c0:c1].astype(F32) + dot(inner[0:size, :], wout[:, c0:c1])
            ).astype(BF16)
        for j in range(OWNERS):
            store = pltpu.make_async_copy(
                result.at[pl.ds(start + count * j, count)],
                out.at[pl.ds(BLOCK * j + inside, count)],
                sem_out.at[half * OWNERS + j],
            )
            store.start()
            stores.append(store)

    for slot in range(8):
        ref_copy(slot).wait_send()

    for half in range(2):

        @pl.loop(1, FRAME)
        def _(d):
            @pl.when(is_owner(d))
            def _():
                go_copy(half, d).wait_send()

            @pl.when(me_f < OWNERS)
            def _():
                back_copy(half, d).wait_send()

    for store in stores:
        store.wait()


def time_embedding(steps):
    half = D // 2
    freqs = jnp.exp(-math.log(10000.0) * jnp.arange(half, dtype=F32) / half)
    angles = steps.astype(F32)[:, None] * freqs[None, :]
    return jnp.concatenate([jnp.cos(angles), jnp.sin(angles)], axis=-1).astype(BF16)


def per_device(
    latents, timestep, ref_features, norm_gains, w_spatial, w_temporal, w_time, w_in, w_out
):
    emb = time_embedding(timestep)
    vmem = pl.BlockSpec(memory_space=pltpu.VMEM)
    hbm = pl.BlockSpec(memory_space=pl.ANY)
    sems = pltpu.SemaphoreType.DMA
    result = pl.pallas_call(
        body,
        out_shape=jax.ShapeDtypeStruct((ROWS, D), BF16),
        in_specs=[hbm, vmem, vmem, vmem, hbm, hbm, hbm, hbm, hbm],
        out_specs=hbm,
        scratch_shapes=[
            pltpu.VMEM((ROWS, D), BF16),
            pltpu.VMEM((ROWS, D), BF16),
            pltpu.VMEM((ROWS, D), BF16),
            pltpu.VMEM((ROWS, WIDE), BF16),
            pltpu.VMEM((WIDE, KEYS_SELF), BF16),
            pltpu.VMEM((KEYS_SELF, WIDE), BF16),
            pltpu.VMEM((REF_PAD, D), BF16),
            pltpu.VMEM((KEYS_REF, D), BF16),
            pltpu.VMEM((WIDE, KEYS_REF), BF16),
            pltpu.VMEM((KEYS_REF, WIDE), BF16),
            pltpu.VMEM((ROWS, WIDE), F32),
            pltpu.VMEM((2, ROWS, KEYS_REF), F32),
            pltpu.VMEM((512, WIDE), BF16),
            pltpu.VMEM((D, WIDE), BF16),
            pltpu.VMEM((D, WIDE), BF16),
            pltpu.VMEM((D, WIDE), BF16),
            pltpu.VMEM((WIDE, D), BF16),
            pltpu.VMEM((4, D, D), BF16),
            pltpu.VMEM((4, D, D), BF16),
            pltpu.VMEM((D, 2 * D), BF16),
            pltpu.VMEM((D, 2 * FFH), BF16),
            pltpu.VMEM((FFH, D), BF16),
            pltpu.VMEM((16, 2 * D), F32),
            pltpu.VMEM((PAD, FRAME * PAD), BF16),
            pltpu.VMEM((FRAME * PAD, PAD), BF16),
            pltpu.VMEM((FRAME, 64, D), BF16),
            pltpu.VMEM((FRAME, 48, D), BF16),
            pltpu.VMEM((FRAME, 64, D), BF16),
            pltpu.VMEM((FRAME, 48, D), BF16),
            pltpu.VMEM((ROWS, D), BF16),
            pltpu.VMEM((448, FFH), BF16),
            sems((2 * OWNERS,)),
            sems((8,)),
            sems((2 * OWNERS,)),
            sems((CLIP,)),
            sems((CLIP,)),
            sems((2 * FRAME,)),
            sems((2 * FRAME,)),
            sems((2 * FRAME,)),
            sems((2 * FRAME,)),
        ],
        compiler_params=pltpu.CompilerParams(
            collective_id=0, has_side_effects=True, vmem_limit_bytes=60 * 1024 * 1024
        ),
        name="block",
    )(latents[0], ref_features, emb, norm_gains, w_spatial, w_temporal, w_time, w_in, w_out)
    return result[None]


def solution(mesh):
    placed = (
        P(("clip", "frame"), None, None),
        P(("clip", "frame")),
        P("clip", None),
        P(),
        P(),
        P(),
        P(),
        P(),
        P(),
    )
    return jax.shard_map(
        per_device,
        mesh=mesh,
        in_specs=placed,
        out_specs=P(("clip", "frame"), None, None),
        check_vma=False,
    )
```

```python
import math

import jax
import jax.numpy as jnp
from jax import lax
from jax.experimental import pallas as pl
from jax.experimental.pallas import tpu as pltpu
from jax.sharding import PartitionSpec as P

HEADS = 8
HEAD = 80
D = 640
FFH = 2560
ROWS = 784
PAD = 128
WIDE = HEADS * PAD
CLIP = 16
FRAME = 8
OWNERS = 7
BLOCK = 112
REF = 49
REF_PAD = 64
KEYS_SELF = 768
KEYS_REF = CLIP * REF_PAD
HALVES = ((0, 64, 0), (448, 48, 64))
LOG2E = 1.4426950408889634
FACTOR = LOG2E / math.sqrt(HEAD)
F32 = jnp.float32
BF16 = jnp.bfloat16
MESH = pl.DeviceIdType.MESH


def dot(a, b):
    return jnp.dot(a, b, preferred_element_type=F32)


def norm(wide):
    mean = jnp.mean(wide, axis=-1, keepdims=True)
    centered = wide - mean
    variance = jnp.mean(centered * centered, axis=-1, keepdims=True)
    return centered * lax.rsqrt(variance + 1e-05)


def iota(shape, axis):
    return lax.broadcasted_iota(jnp.int32, shape, axis)


def head_of(column):
    return (column * 52429) >> 22


def attend(rows, size, keys, q, k_t, v, held, floor, finish, per):
    def columns(n):
        return pl.ds(pl.multiple_of(n * PAD, PAD), PAD)

    def scores(n, slot):
        c = columns(n)
        s = dot(q[rows, c], k_t[c, :])
        held[slot, 0:size, 0:keys] = s
        top = jnp.max(s, axis=1, keepdims=True)
        return top if floor is None else jnp.maximum(top, floor(c))

    @pl.loop(0, HEADS // per)
    def _(i):
        top = scores(i * per, 0)
        for n in range(per):
            c = columns(i * per + n)
            later = scores(i * per + n + 1, (n + 1) % 2) if n + 1 < per else None
            weights = jnp.exp2(held[n % 2, 0:size, 0:keys] - top).astype(BF16)
            finish(c, top, dot(weights, v[:, c]))
            top = later


def body(
    lat, ref, emb, gains, w_spatial, w_temporal, w_time, w_in, w_out, out,
    x, first, h, q, k_t, v, ref_stage, ref_all, kr_t, vr, acc, held, attn, wq, wk, wv, wo,
    ws, wt, swap, wtime, win, wout, mod, spread, gather,
    recv_a, recv_b, moved_a, moved_b, ret, inner,
    sem_x, sem_w, sem_out, ref_send, ref_recv, go_send, go_recv, back_send, back_recv,
):
    wtp = (ws.at[1], ws.at[2], ws.at[3], wt.at[0])
    tq, tk, tv, mixed = (w.at[0:512, 0:D] for w in (wq, wk, wv, wtime))
    result = ret

    me_c = lax.axis_index("clip")
    me_f = lax.axis_index("frame")

    loads_x = []
    for half, (start, count, inside) in enumerate(HALVES):
        for j in range(OWNERS):
            loads_x.append(
                pltpu.make_async_copy(
                    lat.at[pl.ds(BLOCK * j + inside, count)],
                    x.at[pl.ds(start + count * j, count)],
                    sem_x.at[half * OWNERS + j],
                )
            )
    loads_ws = [pltpu.make_async_copy(w_spatial.at[i], ws.at[i], sem_w.at[4 + i]) for i in range(4)]
    load_wtime = pltpu.make_async_copy(w_time, wtime, sem_w.at[0])
    load_wt = pltpu.make_async_copy(w_temporal, wt, sem_w.at[1])
    load_win = pltpu.make_async_copy(w_in, win, sem_w.at[2])
    load_wout = pltpu.make_async_copy(w_out, wout, sem_w.at[3])
    for load in loads_x:
        load.start()
    for load in loads_ws:
        load.start()

    ref_stage[...] = jnp.zeros_like(ref_stage)
    ref_stage[0:REF, :] = ref[...]

    z_hi, y, core = lax.div(me_c, 8), lax.rem(lax.div(me_c, 2), 4), lax.rem(me_c, 2)
    other_frame = me_f + 1 - 2 * lax.rem(me_f, 2)
    sibling = me_c + 1 - 2 * core
    routes = [(0, dy) for dy in (1, 2, 3)] + [(1, dy) for dy in range(4)]

    def clip_of(far, dy, at_core):
        half = (1 - z_hi) if far else z_hi
        return half * 8 + lax.rem(y + dy, 4) * 2 + at_core

    targets = [(clip_of(far, dy, core), other_frame if far else me_f) for far, dy in routes]
    targets.append((sibling, me_f))
    barrier = pltpu.get_barrier_semaphore()
    for clip, frame in targets:
        pl.semaphore_signal(
            barrier, inc=1, device_id={"clip": clip, "frame": frame}, device_id_type=MESH
        )

    @pl.loop(1, FRAME)
    def _(d):
        pl.semaphore_signal(
            barrier,
            inc=1,
            device_id={"clip": me_c, "frame": lax.rem(me_f + d, FRAME)},
            device_id_type=MESH,
        )

    pl.semaphore_wait(barrier, len(targets) + FRAME - 1)

    def ref_rows(clip):
        return ref_all.at[pl.ds(pl.multiple_of(clip * REF_PAD, REF_PAD), REF_PAD)]

    def ref_copy(slot):
        clip, frame = targets[slot]
        return pltpu.make_async_remote_copy(
            src_ref=ref_stage,
            dst_ref=ref_rows(me_c),
            send_sem=ref_send.at[slot],
            recv_sem=ref_recv.at[slot],
            device_id={"clip": clip, "frame": frame},
            device_id_type=MESH,
        )

    def ref_forward(slot):
        far, dy = routes[slot]
        piece = ref_rows(clip_of(far, 4 - dy, core))
        return pltpu.make_async_remote_copy(
            src_ref=piece,
            dst_ref=piece,
            send_sem=ref_send.at[8 + slot],
            recv_sem=ref_recv.at[8 + slot],
            device_id={"clip": sibling, "frame": me_f},
            device_id_type=MESH,
        )

    for slot in range(8):
        ref_copy(slot).start()

    ref_all[pl.ds(pl.multiple_of(me_c * REF_PAD, REF_PAD), REF_PAD), :] = ref_stage[...]

    wq[...] = jnp.zeros_like(wq)
    wk[...] = jnp.zeros_like(wk)
    wv[...] = jnp.zeros_like(wv)
    wo[...] = jnp.zeros_like(wo)

    column = iota((D, D), 1)
    source = HEAD * ((column & (PAD - 1)) >> 4) + 16 * (column >> 7) + (column & 15)
    swap[...] = (iota((D, D), 0) == source).astype(F32).astype(BF16)
    place = iota((FRAME * PAD, PAD), 0)
    pair = FRAME * (place >> 7) + ((place & (PAD - 1)) >> 4)
    gather[...] = ((iota((FRAME * PAD, PAD), 1) & 63) == pair).astype(F32).astype(BF16)
    place = iota((PAD, FRAME * PAD), 1)
    pair = FRAME * (place >> 7) + ((place & (PAD - 1)) >> 4)
    spread[...] = (iota((PAD, FRAME * PAD), 0) == pair).astype(F32).astype(BF16)

    for load in loads_x:
        load.wait()

    @pl.loop(0, ROWS // BLOCK)
    def _(i):
        rows = pl.ds(pl.multiple_of(i * BLOCK, BLOCK), BLOCK)
        h[rows, :] = (norm(x[rows, :].astype(F32)) * gains[0:1, :]).astype(BF16)

    for i, target in enumerate((wq, wk, wv)):
        loads_ws[i].wait()
        for n in range(HEADS):
            target[:, PAD * n : PAD * n + HEAD] = ws[i, :, HEAD * n : HEAD * n + HEAD]
    loads_ws[3].wait()
    for n in range(HEADS):
        wo[PAD * n : PAD * n + HEAD, :] = ws[3, HEAD * n : HEAD * n + HEAD, :]
    load_wtime.start()
    load_wt.start()
    load_win.start()
    load_wout.start()

    for j in range(WIDE // 256):
        c = pl.ds(j * 256, 256)
        lane = iota((1, 256), 1) & (PAD - 1)
        q[:, c] = jnp.where(lane == HEAD, 1.0, dot(h[...], wq[:, c]) * FACTOR).astype(BF16)
        k_t[c, :] = dot(h[0:KEYS_SELF, :], wk[:, c]).astype(BF16).T
        v[:, c] = jnp.where(lane == HEAD, 1.0, dot(h[0:KEYS_SELF, :], wv[:, c])).astype(BF16)

    def attend_own(half):
        start, count, _ = HALVES[half]
        rows = pl.ds(start, count * OWNERS)

        def own(c, top, o):
            acc[rows, c] = jnp.where(iota((1, PAD), 1) == HEAD + 1, top, o)

        attend(rows, count * OWNERS, KEYS_SELF, q, k_t, v, held, None, own, 4)

    for slot in range(7):
        ref_copy(slot).wait_recv()
        ref_forward(slot).start()
    attend_own(0)

    load_wtime.wait()
    mod[...] = dot(jnp.broadcast_to(emb[...], (16, D)), wtime[...])

    ref_copy(7).wait_recv()
    for slot in range(7):
        ref_forward(slot).wait()

    row = iota((PAD, 16), 0)
    tail = iota((PAD, 16), 1)
    place = ((row < REF_PAD) & (row == tail + REF)) | ((row == REF_PAD + REF) & (tail == 15))
    placed = dot(place.astype(F32).astype(BF16), h[KEYS_SELF:ROWS, :])
    ref_all[0:PAD, :] = (ref_all[0:PAD, :].astype(F32) + placed).astype(BF16)

    for j in range(WIDE // 256):
        c = pl.ds(j * 256, 256)
        lane = iota((1, 256), 1) & (PAD - 1)
        key = iota((KEYS_REF, 1), 0)
        valid = ((key & (REF_PAD - 1)) < REF) | (key < REF_PAD) | (key == REF_PAD + REF)
        mask = jnp.where(valid, 0.0, -1e30)
        kr_t[c, :] = jnp.where(lane == HEAD, mask, dot(ref_all[...], wk[:, c])).astype(BF16).T
        vr[:, c] = jnp.where(lane == HEAD, 1.0, dot(ref_all[...], wv[:, c])).astype(BF16)

    def go_copy(half, d):
        start, count, _ = HALVES[half]
        target = lax.rem(me_f + d, FRAME)
        block = lax.min(target, OWNERS - 1)
        return pltpu.make_async_remote_copy(
            src_ref=h.at[pl.ds(pl.multiple_of(start + block * count, 16), count)],
            dst_ref=(recv_a, recv_b)[half].at[me_f],
            send_sem=go_send.at[half * FRAME + d],
            recv_sem=go_recv.at[half * FRAME + d],
            device_id={"clip": me_c, "frame": target},
            device_id_type=MESH,
        )

    def is_owner(d):
        return lax.rem(me_f + d, FRAME) < OWNERS

    def comes_from_owner(d):
        return lax.rem(me_f + FRAME - d, FRAME) < OWNERS

    for half, (start, count, _) in enumerate(HALVES):
        size = count * OWNERS
        rows = pl.ds(start, size)

        if half == 1:
            attend_own(1)

        def own_top(c):
            return acc[rows, c][:, HEAD + 1 : HEAD + 2]

        def merge(c, top, o):
            before = acc[rows, c]
            o = o + before * jnp.exp2(before[:, HEAD + 1 : HEAD + 2] - top)
            attn[0:size, c] = (o * (1.0 / o[:, HEAD : HEAD + 1])).astype(BF16)

        attend(rows, size, KEYS_REF, q, kr_t, vr, held, own_top, merge, 8)

        for c0, c1 in ((0, 256), (256, 512), (512, D)):
            first[rows, c0:c1] = (
                x[rows, c0:c1].astype(F32) + dot(attn[0:size, :], wo[:, c0:c1])
            ).astype(BF16)

        @pl.loop(1, FRAME + 1)
        def _(d):
            @pl.when(is_owner(d))
            def _():
                block = lax.min(lax.rem(me_f + d, FRAME), OWNERS - 1)
                part = pl.ds(pl.multiple_of(start + block * count, 16), count)
                normed = norm(first[part, :].astype(F32)) * gains[1:2, :]
                h[part, :] = (normed * (1.0 + mod[0:1, D:]) + mod[0:1, :D]).astype(BF16)

                @pl.when(d < FRAME)
                def _():
                    go_copy(half, d).start()

        @pl.when(me_f < OWNERS)
        def _():
            (recv_a, recv_b)[half][me_f] = h[
                pl.ds(pl.multiple_of(start + lax.min(me_f, OWNERS - 1) * count, 16), count), :
            ]

    def back_copy(half, d):
        start, count, _ = HALVES[half]
        target = lax.rem(me_f + d, FRAME)
        return pltpu.make_async_remote_copy(
            src_ref=(moved_a, moved_b)[half].at[target],
            dst_ref=ret.at[pl.ds(pl.multiple_of(start + lax.min(me_f, OWNERS - 1) * count, 16), count)],
            send_sem=back_send.at[half * FRAME + d],
            recv_sem=back_recv.at[half * FRAME + d],
            device_id={"clip": me_c, "frame": target},
            device_id_type=MESH,
        )

    load_wt.wait()
    for i in range(3):
        for c0, c1 in ((0, 256), (256, 512), (512, D)):
            wtp[i][:, c0:c1] = dot(wt[i], swap[:, c0:c1]).astype(BF16)
    for n in range(HEADS):
        for r in range(D // PAD):
            wtp[3][PAD * r + 16 * n : PAD * r + 16 * n + 16, :] = wt[
                3, HEAD * n + 16 * r : HEAD * n + 16 * r + 16, :
            ]
    @pl.when(me_f < OWNERS)
    def _():
        for half, (start, count, _) in enumerate(HALVES):
            size = count * FRAME
            recv = (recv_a, recv_b)[half]
            moved = (moved_a, moved_b)[half]

            @pl.loop(1, FRAME)
            def _(d):
                go_copy(half, d).wait_recv()

            for c0, c1 in ((0, 256), (256, 512), (512, D)):
                states = recv[...].reshape(size, D)
                tq[0:size, c0:c1] = (dot(states, wtp[0][:, c0:c1]) * FACTOR).astype(BF16)
                tk[0:size, c0:c1] = dot(states, wtp[1][:, c0:c1]).astype(BF16)
                tv[0:size, c0:c1] = dot(states, wtp[2][:, c0:c1]).astype(BF16)

            def at(f, i):
                return pl.ds(pl.multiple_of(f * count + 16 * i, 16), 16)

            @pl.loop(0, count // 16)
            def _(i):
                for f in range(FRAME):
                    queries = tq[at(f, i), :]
                    for g in range(FRAME):
                        pairs = queries * tk[at(g, i), :]
                        part = pairs[:, 0:PAD]
                        for r in range(1, D // PAD):
                            part = part + pairs[:, PAD * r : PAD * r + PAD]
                        attn[at(f, i), PAD * g : PAD * g + PAD] = part

            s = dot(attn[0:size, :], gather[...])
            top = s
            for shift in (8, 16, 32):
                top = jnp.maximum(top, pltpu.roll(top, shift, 1))
            e = jnp.exp2(s - top)
            total = e
            for shift in (8, 16, 32):
                total = total + pltpu.roll(total, shift, 1)
            weights = (e / total).astype(BF16)
            for c0 in range(0, FRAME * PAD, 256):
                attn[0:size, c0 : c0 + 256] = dot(weights, spread[:, c0 : c0 + 256]).astype(BF16)

            @pl.loop(0, count // 16)
            def _(i):
                for f in range(FRAME):
                    for r in range(D // PAD):
                        c = slice(PAD * r, PAD * r + PAD)
                        terms = [
                            attn[at(f, i), PAD * g : PAD * g + PAD] * tv[at(g, i), c]
                            for g in range(FRAME)
                        ]
                        while len(terms) > 1:
                            terms = [a + b for a, b in zip(terms[0::2], terms[1::2])]
                        mixed[at(f, i), c] = terms[0]

            for c0, c1 in ((0, 256), (256, 512), (512, D)):
                moved[:, :, c0:c1] = (
                    dot(mixed[0:size, :], wtp[3][:, c0:c1]).astype(BF16).reshape(FRAME, count, c1 - c0)
                )

            @pl.loop(1, FRAME)
            def _(d):
                back_copy(half, d).start()

            ret[pl.ds(pl.multiple_of(start + lax.min(me_f, OWNERS - 1) * count, 16), count), :] = moved[
                me_f
            ]

    load_win.wait()
    load_wout.wait()
    stores = []
    for half, (start, count, inside) in enumerate(HALVES):
        size = count * OWNERS
        rows = pl.ds(start, size)

        @pl.loop(0, FRAME)
        def _(d):
            @pl.when(comes_from_owner(d))
            def _():
                @pl.when(d > 0)
                def _():
                    back_copy(half, d).wait_recv()

                block = lax.min(lax.rem(me_f + FRAME - d, FRAME), OWNERS - 1)
                part = pl.ds(pl.multiple_of(start + block * count, 16), count)
                second = (first[part, :].astype(F32) + ret[part, :].astype(F32)).astype(BF16)
                x[part, :] = second
                first[part, :] = (norm(second.astype(F32)) * gains[2:3, :]).astype(BF16)

        @pl.loop(0, 2)
        def _(i):
            for j in range(FFH // 512):
                c = pl.ds(pl.multiple_of(i * (FFH // 2) + 256 * j, 256), 256)
                g = pl.ds(pl.multiple_of(FFH + i * (FFH // 2) + 256 * j, 256), 256)
                value = dot(first[rows, :], win[:, c])
                gate = dot(first[rows, :], win[:, g])
                gelu = 0.5 * gate * (1.0 + lax.erf(gate * (1.0 / math.sqrt(2.0))))
                inner[0:size, c] = (value * gelu).astype(BF16)

        for c0, c1 in ((0, 256), (256, 512), (512, D)):
            result[rows, c0:c1] = (
                x[rows, c0:c1].astype(F32) + dot(inner[0:size, :], wout[:, c0:c1])
            ).astype(BF16)
        for j in range(OWNERS):
            store = pltpu.make_async_copy(
                result.at[pl.ds(start + count * j, count)],
                out.at[pl.ds(BLOCK * j + inside, count)],
                sem_out.at[half * OWNERS + j],
            )
            store.start()
            stores.append(store)

    for slot in range(8):
        ref_copy(slot).wait_send()

    for half in range(2):

        @pl.loop(1, FRAME)
        def _(d):
            @pl.when(is_owner(d))
            def _():
                go_copy(half, d).wait_send()

            @pl.when(me_f < OWNERS)
            def _():
                back_copy(half, d).wait_send()

    for store in stores:
        store.wait()


def time_embedding(steps):
    half = D // 2
    freqs = jnp.exp(-math.log(10000.0) * jnp.arange(half, dtype=F32) / half)
    angles = steps.astype(F32)[:, None] * freqs[None, :]
    return jnp.concatenate([jnp.cos(angles), jnp.sin(angles)], axis=-1).astype(BF16)


def per_device(
    latents, timestep, ref_features, norm_gains, w_spatial, w_temporal, w_time, w_in, w_out
):
    emb = time_embedding(timestep)
    vmem = pl.BlockSpec(memory_space=pltpu.VMEM)
    hbm = pl.BlockSpec(memory_space=pl.ANY)
    sems = pltpu.SemaphoreType.DMA
    result = pl.pallas_call(
        body,
        out_shape=jax.ShapeDtypeStruct((ROWS, D), BF16),
        in_specs=[hbm, vmem, vmem, vmem, hbm, hbm, hbm, hbm, hbm],
        out_specs=hbm,
        scratch_shapes=[
            pltpu.VMEM((ROWS, D), BF16),
            pltpu.VMEM((ROWS, D), BF16),
            pltpu.VMEM((ROWS, D), BF16),
            pltpu.VMEM((ROWS, WIDE), BF16),
            pltpu.VMEM((WIDE, KEYS_SELF), BF16),
            pltpu.VMEM((KEYS_SELF, WIDE), BF16),
            pltpu.VMEM((REF_PAD, D), BF16),
            pltpu.VMEM((KEYS_REF, D), BF16),
            pltpu.VMEM((WIDE, KEYS_REF), BF16),
            pltpu.VMEM((KEYS_REF, WIDE), BF16),
            pltpu.VMEM((ROWS, WIDE), F32),
            pltpu.VMEM((2, ROWS, KEYS_REF), F32),
            pltpu.VMEM((512, WIDE), BF16),
            pltpu.VMEM((D, WIDE), BF16),
            pltpu.VMEM((D, WIDE), BF16),
            pltpu.VMEM((D, WIDE), BF16),
            pltpu.VMEM((WIDE, D), BF16),
            pltpu.VMEM((4, D, D), BF16),
            pltpu.VMEM((4, D, D), BF16),
            pltpu.VMEM((D, D), BF16),
            pltpu.VMEM((D, 2 * D), BF16),
            pltpu.VMEM((D, 2 * FFH), BF16),
            pltpu.VMEM((FFH, D), BF16),
            pltpu.VMEM((16, 2 * D), F32),
            pltpu.VMEM((PAD, FRAME * PAD), BF16),
            pltpu.VMEM((FRAME * PAD, PAD), BF16),
            pltpu.VMEM((FRAME, 64, D), BF16),
            pltpu.VMEM((FRAME, 48, D), BF16),
            pltpu.VMEM((FRAME, 64, D), BF16),
            pltpu.VMEM((FRAME, 48, D), BF16),
            pltpu.VMEM((ROWS, D), BF16),
            pltpu.VMEM((448, FFH), BF16),
            sems((2 * OWNERS,)),
            sems((8,)),
            sems((2 * OWNERS,)),
            sems((CLIP,)),
            sems((CLIP,)),
            sems((2 * FRAME,)),
            sems((2 * FRAME,)),
            sems((2 * FRAME,)),
            sems((2 * FRAME,)),
        ],
        compiler_params=pltpu.CompilerParams(
            collective_id=0, has_side_effects=True, vmem_limit_bytes=60 * 1024 * 1024
        ),
        name="block",
    )(latents[0], ref_features, emb, norm_gains, w_spatial, w_temporal, w_time, w_in, w_out)
    return result[None]


def solution(mesh):
    placed = (
        P(("clip", "frame"), None, None),
        P(("clip", "frame")),
        P("clip", None),
        P(),
        P(),
        P(),
        P(),
        P(),
        P(),
    )
    return jax.shard_map(
        per_device,
        mesh=mesh,
        in_specs=placed,
        out_specs=P(("clip", "frame"), None, None),
        check_vma=False,
    )
```
